256 devices in a mesh: section: 32 (over z_hi, x, core), tensor: 8 (over z_lo, y).
Axes of the slice: x: 4, y: 4, z: 8 (z_hi: 4, z_lo: 2; z = z_hi * 2 + z_lo), core: 2. Of those that a mesh axis runs over, the one named last changes fastest.
Arguments:
- acts: bfloat16 [32, 512, 4096], P('section', 'tensor'), may hold values from -6 to 6
- next_grad: bfloat16 [32, 512, 4096], P('section', 'tensor'), may hold values from -6 to 6
- head_grad: bfloat16 [512, 4096], P('tensor'), may hold values from -6 to 6
- blocks: bfloat16 [32, 768, 12288], P('section', 'tensor'), may hold values from -0.875 to 0.875
- block_row: int32 [32, 768], P('section', 'tensor'), may hold values from 0 to 63, as said below
- block_col: int32 [32, 768], P('section', 'tensor'), may hold values from 0 to 55, as said below
- live: int32 [32, 8], P('section', 'tensor'), may hold values from 12 to 96, as said below
Outputs:
- input_grad: bfloat16 [32, 512, 4096], P('section', 'tensor')
- block_grads: bfloat16 [32, 768, 12288], P('section', 'tensor')
The draws below stay inside these ranges and needn't reach their ends.
Inputs may be any that keep to these rules, and one draw needn't show every extreme that they name: `block_row`: within one shard of one section the live slots name distinct blocks. `block_col`: within one shard of one section the live slots name distinct blocks. Every section has a shard with all 96 slots live.
All inputs are finite; a program needn't handle non-finite values.
Results may differ from the reference program's by a relative error of at most 0.023.
Values may be sent and summed in bfloat16 or wider, within the bound.
A program may use at most 192 MiB of HBM per device.

```python
import jax
import jax.numpy as jnp
from jax import lax

D = 4096
CAP = 96
SECTIONS = 32
TOKENS = 512
FBD = 56
SLOTS = 768
N_TENSOR = 8


def slot_ids(key):
    keys = jax.random.split(key, SECTIONS * N_TENSOR)
    picked = jax.vmap(lambda subkey: jax.random.permutation(subkey, D // 64 * FBD)[:CAP])(keys)
    return picked.reshape(SECTIONS, N_TENSOR * CAP).astype(jnp.int32)


def draw_block_row(key, part):
    picked = slot_ids(key)
    return (picked // FBD).astype(jnp.int32)


def draw_block_col(key, part):
    picked = slot_ids(key)
    return (picked % FBD).astype(jnp.int32)


def draw_live(key, part):
    key = jax.random.fold_in(key, 5)
    first_key, second_key = jax.random.split(key)
    lowest = max(1, CAP // 8)
    counts = jax.random.randint(first_key, (SECTIONS, N_TENSOR), lowest, CAP // 2 + 1)
    heavy = jax.random.randint(second_key, (SECTIONS,), 0, N_TENSOR)
    counts = jnp.where(jnp.arange(N_TENSOR)[None, :] == heavy[:, None], CAP, counts)
    return counts.astype(jnp.int32)


def block_scale(stream_key, dims, cuts, smallest, top_value):
    def one(position, blocks):
        steps = jax.random.uniform(jax.random.fold_in(jax.random.fold_in(stream_key, 6), position), (blocks,), jnp.float32, smallest / len(cuts), top_value / len(cuts))
        return jnp.repeat(jnp.exp(steps), dims[position] // blocks).reshape((-1,) + (1,) * (len(dims) - position - 1))

    factor_of = one(*cuts[0])
    for cut in cuts[1:]:
        factor_of = factor_of * one(*cut)
    return factor_of


def bell_draw(key, dims, spread, most, cuts=(), held_as=jnp.bfloat16):
    values = jax.random.normal(key, dims, jnp.float32) * spread
    if len(cuts) > 0:
        values = block_scale(key, dims, cuts, -0.22, 0.18) * values
    return jnp.clip(values, min=-most, max=most).astype(held_as)


def setup_inputs(seed: int = 0) -> dict:
    arg_keys = jax.random.split(jax.random.key(seed), 8)
    acts = bell_draw(arg_keys[0], (SECTIONS, TOKENS, D), 1.0, 6.0, ((0, 32), (1, 8)))
    next_grad = bell_draw(arg_keys[1], (SECTIONS, TOKENS, D), 1.0, 6.0, ((0, 32), (1, 8)))
    head_grad = bell_draw(arg_keys[2], (TOKENS, D), 1.0, 6.0, ((0, 8),))
    blocks = bell_draw(arg_keys[3], (SECTIONS, SLOTS, 12288), (32 * CAP // FBD) ** -0.5, 0.875, ((0, 32), (1, 8)))
    block_row = draw_block_row(jax.random.fold_in(arg_keys[7], 71), 0)
    block_col = draw_block_col(jax.random.fold_in(arg_keys[7], 71), 0)
    live = draw_live(jax.random.fold_in(arg_keys[7], 71), 0)
    return {"acts": acts, "next_grad": next_grad, "head_grad": head_grad, "blocks": blocks, "block_row": block_row, "block_col": block_col, "live": live}


def shard_pass(act_blocks, grad_blocks, packed, row_ids, col_ids, live_count):
    capacity = row_ids.shape[0]
    tokens = act_blocks.shape[0]
    row_count = act_blocks.shape[1]
    hp = lax.Precision.HIGHEST
    is_live = jnp.arange(capacity) < live_count
    weights = jnp.where(is_live[:, None], packed, jnp.zeros_like(packed))
    weights = weights.reshape(capacity, 3, 64, 64).astype(jnp.float32)
    x_slot = jnp.take(act_blocks, row_ids, axis=1).astype(jnp.float32)
    dy_slot = jnp.take(grad_blocks, row_ids, axis=1).astype(jnp.float32)
    col_hot = (col_ids[:, None] == jnp.arange(FBD)[None, :]).astype(jnp.float32)
    row_hot = (row_ids[:, None] == jnp.arange(row_count)[None, :]).astype(jnp.float32)
    gate = jnp.einsum('tkf,kc->tcf', jnp.einsum('tkd,kdf->tkf', x_slot, weights[:, 0], precision=hp), col_hot, precision=hp)
    upper = jnp.einsum('tkf,kc->tcf', jnp.einsum('tkd,kdf->tkf', x_slot, weights[:, 1], precision=hp), col_hot, precision=hp)
    hidden_grad = jnp.einsum('tkf,kc->tcf', jnp.einsum('tkd,kfd->tkf', dy_slot, weights[:, 2], precision=hp), col_hot, precision=hp)
    sigmoid_gate = jax.nn.sigmoid(gate)
    activated = gate * sigmoid_gate
    hidden = (activated * upper).astype(jnp.bfloat16)
    gate_grad = (hidden_grad * upper * sigmoid_gate * (1.0 + gate * (1.0 - sigmoid_gate))).astype(jnp.bfloat16)
    up_grad = (hidden_grad * activated).astype(jnp.bfloat16)
    g_slot = jnp.take(gate_grad, col_ids, axis=1).astype(jnp.float32)
    u_slot = jnp.take(up_grad, col_ids, axis=1).astype(jnp.float32)
    h_slot = jnp.take(hidden, col_ids, axis=1).astype(jnp.float32)
    back_slot = jnp.einsum('tkf,kdf->tkd', g_slot, weights[:, 0], precision=hp) + jnp.einsum('tkf,kdf->tkd', u_slot, weights[:, 1], precision=hp)
    shard_part = jnp.einsum('tkd,kr->trd', back_slot, row_hot, precision=hp).reshape(tokens, row_count * 64).astype(jnp.bfloat16)
    grad_gate = jnp.einsum('tkd,tkf->kdf', x_slot, g_slot, precision=hp)
    grad_up = jnp.einsum('tkd,tkf->kdf', x_slot, u_slot, precision=hp)
    grad_down = jnp.einsum('tkf,tkd->kfd', h_slot, dy_slot, precision=hp)
    stacked = jnp.stack([grad_gate, grad_up, grad_down], axis=1) * is_live.astype(jnp.float32)[:, None, None, None]
    return shard_part, stacked.reshape(capacity, 12288).astype(jnp.bfloat16)


def section_pass(inputs):
    acts_one, incoming_one, packed, row_ids, col_ids, counts = inputs
    tokens = acts_one.shape[0]
    shards = counts.shape[0]
    capacity = row_ids.shape[0] // shards
    act_blocks = acts_one.reshape(tokens, -1, 64)
    grad_blocks = incoming_one.reshape(tokens, -1, 64)

    def one_shard(items):
        return shard_pass(act_blocks, grad_blocks, items[0], items[1], items[2], items[3])

    parts, grads = lax.map(one_shard, (packed.reshape(shards, capacity, 12288), row_ids.reshape(shards, capacity), col_ids.reshape(shards, capacity), counts))
    total = jnp.sum(parts.astype(jnp.float32), axis=0)
    input_grad = (incoming_one.astype(jnp.float32) + total).astype(jnp.bfloat16)
    return input_grad, grads.reshape(shards * capacity, 12288)


def reference(acts, next_grad, head_grad, blocks, block_row, block_col, live):
    incoming = jnp.concatenate([next_grad[1:], head_grad[None]], axis=0)
    input_grad, block_grads = lax.map(section_pass, (acts, incoming, blocks, block_row, block_col, live))
    return input_grad, block_grads
```

```python
import functools

import jax
import jax.numpy as jnp
from jax import lax
from jax.experimental import pallas as pl
from jax.experimental.pallas import tpu as pltpu
from jax.sharding import PartitionSpec as P

MESH = pl.DeviceIdType.MESH
BF16 = jnp.bfloat16
F32 = jnp.float32

CAP = 96
ROWS = 64
WIDTH = 4096
TOK = 64
HALF = 256
SLOT = 12288
GROUP = 16
SPLIT = 1664

PARTS = (pl.ds(0, SPLIT), pl.ds(SPLIT, WIDTH - SPLIT))

ORD_C, ROW_C, KEEP_C = 0, 96, 192
ORD_R, POS_R, KEEP_R = 288, 384, 480
LAST_R, POS_K, ROW_K, ALIVE = 576, 640, 736, 832


def slot_order(keys):
    slots = jnp.arange(CAP, dtype=jnp.int32)
    same = keys[:, None] == keys[None, :]
    before = same & (slots[None, :] < slots[:, None])
    smaller = (keys[None, :] < keys[:, None]) | before
    rank = jnp.sum(smaller.astype(jnp.int32), axis=1)
    hot = (rank[None, :] == slots[:, None]).astype(jnp.int32)
    follows = jnp.max(before.astype(jnp.int32), axis=1)
    last = jnp.max(jnp.where(same, rank[None, :], 0), axis=1)
    return rank, hot, follows, last


def index_vector(row, col, live):
    slots = jnp.arange(CAP, dtype=jnp.int32)
    _, hot_c, follows_c, last_c = slot_order(col)
    rank_r, hot_r, follows_r, _ = slot_order(row)

    def in_order(hot, values):
        return jnp.sum(hot * values[None, :], axis=1)

    holds = row[None, :] == jnp.arange(ROWS, dtype=jnp.int32)[:, None]
    last_r = jnp.max(jnp.where(holds, rank_r[None, :] + 1, 0), axis=1)
    last_r = jnp.where(last_r == 0, CAP, last_r - 1)
    return jnp.concatenate(
        [
            in_order(hot_c, slots),
            in_order(hot_c, row),
            in_order(hot_c, follows_c),
            in_order(hot_r, slots),
            in_order(hot_r, last_c),
            in_order(hot_r, follows_r),
            last_r,
            last_c,
            row,
            slots < live,
        ]
    ).astype(jnp.int32)


def kernel(
    sections, index, acts, next_grad, head_grad, blocks, input_grad, block_grads,
    xc, dc, xt, dt, gu, hid, bk, wgu, wgut, wd, raw, part, rsa, rsb, rsz, zsum, s1, s2, acc, acc_b, ig,
    x_send, d_send, x_recv, d_recv, sh_send, a_send, a_recv, b_send, b_recv, z_send, z_recv, loc,
):
    s = lax.axis_index("section")
    t = lax.axis_index("tensor")
    y = lax.rem(t, 4)
    plane = t // 4

    def in_ring(step):
        return (s, plane * 4 + lax.rem(y + step, 4))

    across = (s, (1 - plane) * 4 + y)
    before = (lax.rem(s + sections - 1, sections), t)
    after = (lax.rem(s + 1, sections), t)

    barrier = pltpu.get_barrier_semaphore()
    for peer in (in_ring(1), in_ring(2), in_ring(3), across):
        pl.semaphore_signal(barrier, inc=1, device_id=peer, device_id_type=MESH)
    @pl.when(s < sections - 1)
    def _():
        pl.semaphore_signal(barrier, inc=1, device_id=after, device_id_type=MESH)

    blocks_in = pltpu.make_async_copy(blocks, raw, loc.at[0])
    blocks_in.start()
    own_in = pltpu.make_async_copy(acts, xc.at[0], loc.at[1])
    own_in.start()

    @pl.when(s > 0)
    def _():
        pl.semaphore_wait(barrier, 5)

    @pl.when(s == 0)
    def _():
        pl.semaphore_wait(barrier, 4)

    pending = []

    def send(src, dst, ssem, rsem, peer):
        copy = pltpu.make_async_remote_copy(
            src_ref=src, dst_ref=dst, send_sem=ssem, recv_sem=rsem, device_id=peer, device_id_type=MESH
        )
        copy.start()
        pending.append(copy)

    def arrived(dst, rsem):
        pltpu.make_async_remote_copy(
            src_ref=dst, dst_ref=dst, send_sem=rsem, recv_sem=rsem, device_id=across, device_id_type=MESH
        ).wait_recv()

    for p, cols in enumerate(PARTS):
        shift = pltpu.make_async_remote_copy(
            src_ref=next_grad.at[:, cols], dst_ref=dc.at[0, :, cols], send_sem=sh_send.at[p],
            recv_sem=d_recv.at[0, p], device_id=before, device_id_type=MESH,
        )

        @pl.when(s > 0)
        def _():
            shift.start()

        @pl.when(s == sections - 1)
        def _():
            pltpu.make_async_copy(head_grad.at[:, cols], dc.at[0, :, cols], d_recv.at[0, p]).start()

    def share_own(src, buf, ssem, rsem):
        for p, cols in enumerate(PARTS):
            send(src.at[:, cols], buf.at[4, :, cols], ssem.at[p], rsem.at[4, p], across)
            for step in (1, 3, 2):
                send(
                    src.at[:, cols], buf.at[4 - step, :, cols], ssem.at[2 * step + p], rsem.at[4 - step, p],
                    in_ring(step),
                )

    def pass_on_first(buf, ssem, rsem):
        cols = PARTS[0]
        arrived(buf.at[4, :, cols], rsem.at[4, 0])
        for step in (1, 3, 2):
            send(
                buf.at[4, :, cols], buf.at[8 - step, :, cols], ssem.at[7 + step], rsem.at[8 - step, 0], in_ring(step)
            )

    def pass_on_second(buf, ssem, rsem):
        cols = PARTS[1]
        for step in (1, 3, 2):
            arrived(buf.at[step, :, cols], rsem.at[step, 1])
            send(buf.at[step, :, cols], buf.at[4 + step, :, cols], ssem.at[10 + step], rsem.at[4 + step, 1], across)

    share_own(acts, xc, x_send, x_recv)

    blocks_in.wait()
    low = lax.broadcasted_iota(jnp.int32, (64, 128), 1) < 64
    low32 = lax.broadcasted_iota(jnp.int32, (32, 128), 1) < 64

    def prepare(g, _):
        rows = pl.ds(pl.multiple_of(g * GROUP, GROUP), GROUP)
        for i in range(SLOT // 128):
            s1[pl.ds(i * GROUP, GROUP), :] = raw[rows, pl.ds(i * 128, 128)].astype(F32)
        for j in range(GROUP):
            k = g * GROUP + j
            b = (j % 4) * 192
            for m in range(3):
                v = s1[pl.ds(m * 32 * GROUP + j, 32, stride=GROUP), :]
                turned = pltpu.roll(v, 64, 1)
                even, odd = (turned, v) if m == 1 else (v, turned)
                s2[pl.ds(b + m * 64, 32, stride=2), :] = even
                s2[pl.ds(b + m * 64 + 1, 32, stride=2), :] = odd
            both = jnp.where(low, s2[pl.ds(b, 64), :], s2[pl.ds(b + 64, 64), :])
            alive = index[ALIVE + k].astype(F32)
            both = both * alive
            down = s2[pl.ds(b + 128, 64), :] * alive
            wgu[k] = both.astype(BF16)
            wgut[k] = both.T.astype(BF16)
            wd[k] = down[:, :64].astype(BF16)
        return 0

    lax.fori_loop(0, CAP // GROUP, prepare, 0)
    bk[CAP] = jnp.zeros((64, HALF), BF16)

    for p, cols in enumerate(PARTS):
        arrived(dc.at[0, :, cols], d_recv.at[0, p])
    share_own(dc.at[0], dc, d_send, d_recv)
    pass_on_first(xc, x_send, x_recv)
    pass_on_first(dc, d_send, d_recv)
    pass_on_second(xc, x_send, x_recv)
    pass_on_second(dc, d_send, d_recv)

    def turn(buf, out, pair):
        def step(i, _):
            cols = pl.ds(pl.multiple_of(i * 128, 128), 128)
            tile = jnp.concatenate([buf[2 * pair, :, cols], buf[2 * pair + 1, :, cols]], axis=0)
            tile = tile.T
            out[2 * i, :, pl.ds(pair * 128, 128)] = tile[:64]
            out[2 * i + 1, :, pl.ds(pair * 128, 128)] = tile[64:]
            return 0

        lax.fori_loop(0, WIDTH // 128, step, 0, unroll=4)

    def forward(lanes):
        acc[...] = jnp.zeros_like(acc)

        def step(j, _):
            k, r = index[ORD_C + j], index[ROW_C + j]
            keep = index[KEEP_C + j].astype(F32)
            new = jnp.dot(wgut[k], xt[r, :, lanes], preferred_element_type=F32)
            hg = jnp.dot(wd[k], dt[r, :, lanes], preferred_element_type=F32)
            gate = new[:64] + keep * acc[pl.ds(0, 64), :]
            upper = new[64:] + keep * acc[pl.ds(64, 64), :]
            hg = hg + keep * acc[pl.ds(128, 64), :]
            acc[pl.ds(0, 64), :] = gate
            acc[pl.ds(64, 64), :] = upper
            acc[pl.ds(128, 64), :] = hg
            sg = jax.nn.sigmoid(gate)
            act = gate * sg
            hid[j, :, lanes] = (act * upper).astype(BF16)
            gu[j, pl.ds(0, 64), lanes] = (hg * upper * sg * (1.0 + gate * (1.0 - sg))).astype(BF16)
            gu[j, pl.ds(64, 64), lanes] = (hg * act).astype(BF16)
            return 0

        lax.fori_loop(0, CAP, step, 0, unroll=2)

    def backward(lanes, first_slot):
        acc_b[...] = jnp.zeros_like(acc_b)

        def step(j, _):
            k, p = index[ORD_R + j], index[POS_R + j]
            keep = index[KEEP_R + j].astype(F32)
            new = jnp.dot(wgu[k], gu[p, :, lanes], preferred_element_type=F32)
            new = new + keep * acc_b[...]
            acc_b[...] = new
            bk[j] = new.astype(BF16)
            return 0

        lax.fori_loop(0, CAP, step, 0, unroll=2)

        def place(i, _):
            cols = pl.ds(pl.multiple_of(i * 128, 128), 128)
            both = jnp.concatenate([bk[index[LAST_R + 2 * i]], bk[index[LAST_R + 2 * i + 1]]], axis=0)
            for q in range(2):
                tile = both[:, q * 128:(q + 1) * 128].T
                part[first_slot + 2 * q, :, cols] = tile[:64]
                part[first_slot + 2 * q + 1, :, cols] = tile[64:]
            return 0

        lax.fori_loop(0, ROWS // 2, place, 0, unroll=2)

    own_in.wait()
    for step in (1, 2, 3):
        arrived(xc.at[step, :, PARTS[0]], x_recv.at[step, 0])
    turn(xc, xt, 0)
    turn(xc, xt, 1)
    for step in (1, 2, 3):
        arrived(dc.at[step, :, PARTS[0]], d_recv.at[step, 0])
    turn(dc, dt, 0)
    turn(dc, dt, 1)
    forward(pl.ds(0, HALF))
    backward(pl.ds(0, HALF), 0)
    for step in (1, 3, 2):
        send(part.at[step], rsa.at[3 - step], a_send.at[step - 1], a_recv.at[3 - step], in_ring(step))

    def rest(buf, rsem):
        arrived(buf.at[4, :, PARTS[1]], rsem.at[4, 1])
        for step in (1, 2, 3):
            for p in range(2):
                arrived(buf.at[4 + step, :, PARTS[p]], rsem.at[4 + step, p])

    rest(xc, x_recv)
    turn(xc, xt, 2)
    turn(xc, xt, 3)
    rest(dc, d_recv)
    turn(dc, dt, 2)
    turn(dc, dt, 3)
    forward(pl.ds(HALF, HALF))
    backward(pl.ds(HALF, HALF), 4)
    for step in (1, 3, 2):
        send(part.at[4 + step], rsb.at[3 - step], b_send.at[step - 1], b_recv.at[3 - step], in_ring(step))

    def grads(g, _):
        for j in range(GROUP):
            k = g * GROUP + j
            p, r = index[POS_K + k], index[ROW_K + k]
            alive = index[ALIVE + k].astype(F32)
            turned = (((1,), (1,)), ((), ()))
            d_both = lax.dot_general(xt[r], gu[p], turned, preferred_element_type=F32)
            d_down = lax.dot_general(hid[p], dt[r], turned, preferred_element_type=F32)
            b = (j % 4) * 192
            s2[pl.ds(b, 64), :] = d_both * alive
            s2[pl.ds(b + 64, 64), pl.ds(0, 64)] = d_down * alive
            even, odd = s2[pl.ds(b, 32, stride=2), :], s2[pl.ds(b + 1, 32, stride=2), :]
            d_even, d_odd = s2[pl.ds(b + 64, 32, stride=2), :], s2[pl.ds(b + 65, 32, stride=2), :]
            s1[pl.ds(j, 32, stride=GROUP), :] = jnp.where(low32, even, pltpu.roll(odd, 64, 1))
            s1[pl.ds(32 * GROUP + j, 32, stride=GROUP), :] = jnp.where(low32, pltpu.roll(even, 64, 1), odd)
            s1[pl.ds(64 * GROUP + j, 32, stride=GROUP), :] = jnp.where(low32, d_even, pltpu.roll(d_odd, 64, 1))
        rows = pl.ds(pl.multiple_of(g * GROUP, GROUP), GROUP)
        for i in range(SLOT // 128):
            raw[rows, pl.ds(i * 128, 128)] = s1[pl.ds(i * GROUP, GROUP), :].astype(BF16)
        return 0

    lax.fori_loop(0, CAP // GROUP, grads, 0)
    blocks_out = pltpu.make_async_copy(raw, block_grads, loc.at[2])
    blocks_out.start()

    tiles = [(pl.ds(a, 16), pl.ds(b, 512)) for a in range(0, TOK, 16) for b in range(0, WIDTH, 512)]
    for n in range(3):
        arrived(rsb.at[n], b_recv.at[n])
    for rows, cols in tiles:
        total = part[4, rows, cols].astype(F32)
        for n in range(3):
            total = total + rsb[n, rows, cols].astype(F32)
        zsum[rows, cols] = total.astype(BF16)
    send(zsum, rsz, z_send, z_recv, across)
    for n in range(3):
        arrived(rsa.at[n], a_recv.at[n])
    arrived(rsz, z_recv)
    for rows, cols in tiles:
        total = part[0, rows, cols].astype(F32)
        for n in range(3):
            total = total + rsa[n, rows, cols].astype(F32)
        total = total + rsz[rows, cols].astype(F32)
        ig[rows, cols] = (dc[0, rows, cols].astype(F32) + total).astype(BF16)
    ig_out = pltpu.make_async_copy(ig, input_grad, loc.at[3])
    ig_out.start()

    for copy in pending:
        copy.wait_send()
    for p, cols in enumerate(PARTS):
        @pl.when(s > 0)
        def _():
            pltpu.make_async_remote_copy(
                src_ref=next_grad.at[:, cols], dst_ref=dc.at[0, :, cols], send_sem=sh_send.at[p],
                recv_sem=d_recv.at[0, p], device_id=before, device_id_type=MESH,
            ).wait_send()
    blocks_out.wait()
    ig_out.wait()


def per_device(sections, acts, next_grad, head_grad, blocks, block_row, block_col, live):
    index = index_vector(block_row[0], block_col[0], live[0])
    dma = pltpu.SemaphoreType.DMA
    any_space = pl.BlockSpec(memory_space=pl.ANY)
    input_grad, block_grads = pl.pallas_call(
        functools.partial(kernel, sections),
        out_shape=(
            jax.ShapeDtypeStruct((TOK, WIDTH), BF16),
            jax.ShapeDtypeStruct((CAP, SLOT), BF16),
        ),
        in_specs=[pl.BlockSpec(memory_space=pltpu.SMEM)] + [any_space] * 4,
        out_specs=(any_space, any_space),
        scratch_shapes=[
            pltpu.VMEM((8, TOK, WIDTH), BF16),
            pltpu.VMEM((8, TOK, WIDTH), BF16),
            pltpu.VMEM((ROWS, 64, 2 * HALF), BF16),
            pltpu.VMEM((ROWS, 64, 2 * HALF), BF16),
            pltpu.VMEM((CAP, 128, 2 * HALF), BF16),
            pltpu.VMEM((CAP, 64, 2 * HALF), BF16),
            pltpu.VMEM((CAP + 1, 64, HALF), BF16),
            pltpu.VMEM((CAP, 64, 128), BF16),
            pltpu.VMEM((CAP, 128, 64), BF16),
            pltpu.VMEM((CAP, 64, 64), BF16),
            pltpu.VMEM((CAP, SLOT), BF16),
            pltpu.VMEM((8, TOK, WIDTH), BF16),
            pltpu.VMEM((3, TOK, WIDTH), BF16),
            pltpu.VMEM((3, TOK, WIDTH), BF16),
            pltpu.VMEM((TOK, WIDTH), BF16),
            pltpu.VMEM((TOK, WIDTH), BF16),
            pltpu.VMEM((SLOT // 128 * GROUP, 128), F32),
            pltpu.VMEM((4 * 192, 128), F32),
            pltpu.VMEM((192, HALF), F32),
            pltpu.VMEM((64, HALF), F32),
            pltpu.VMEM((TOK, WIDTH), BF16),
            dma((14,)),
            dma((14,)),
            dma((8, 2)),
            dma((8, 2)),
            dma((2,)),
            dma((3,)),
            dma((3,)),
            dma((3,)),
            dma((3,)),
            dma,
            dma,
            dma((4,)),
        ],
        compiler_params=pltpu.CompilerParams(
            collective_id=0, has_side_effects=True, vmem_limit_bytes=63 * 2**20
        ),
    )(index, acts[0], next_grad[0], head_grad, blocks[0])
    return input_grad[None], block_grads[None]


def solution(mesh):
    return jax.shard_map(
        functools.partial(per_device, mesh.shape["section"]),
        mesh=mesh,
        in_specs=(
            P("section", "tensor", None),
            P("section", "tensor", None),
            P("tensor", None),
            P("section", "tensor", None),
            P("section", "tensor"),
            P("section", "tensor"),
            P("section", "tensor"),
        ),
        out_specs=(P("section", "tensor", None), P("section", "tensor", None)),
        check_vma=False,
    )
```

```python
import functools

import jax
import jax.numpy as jnp
from jax import lax
from jax.experimental import pallas as pl
from jax.experimental.pallas import tpu as pltpu
from jax.sharding import PartitionSpec as P

MESH = pl.DeviceIdType.MESH
BF16 = jnp.bfloat16
F32 = jnp.float32

CAP = 96
ROWS = 64
WIDTH = 4096
TOK = 64
HALF = 256
SLOT = 12288
GROUP = 16
SPLIT = 2048
REST = WIDTH - SPLIT

PARTS = (pl.ds(0, SPLIT), pl.ds(SPLIT, REST))
HALVES = (
    (pl.ds(0, SPLIT // 2), pl.ds(SPLIT // 2, SPLIT // 2)),
    (pl.ds(SPLIT, REST // 2), pl.ds(SPLIT + REST // 2, REST // 2)),
)

ORD_C, ROW_C, KEEP_C, ORD_R, POS_R, KEEP_R, LAST_R, POS_K, ROW_K, ALIVE = range(10)
QUARTERS = tuple(pl.ds(n * WIDTH // 4, WIDTH // 4) for n in range(4))


def fill_table(live_ref, row_ref, col_ref, table):
    table[...] = jnp.zeros_like(table)
    lane = lax.broadcasted_iota(jnp.int32, (CAP, CAP), 1).astype(F32)
    sub = lax.broadcasted_iota(jnp.int32, (CAP, CAP), 0).astype(F32)
    one, none = jnp.ones((CAP, CAP), F32), jnp.zeros((CAP, CAP), F32)

    def both_ways(ref):
        along = jnp.broadcast_to(ref[...].astype(F32), (CAP, CAP))
        down = jnp.sum(jnp.where(lane == sub, along, none), axis=1, keepdims=True)
        return along, jnp.broadcast_to(down, (CAP, CAP))

    def sort(along, down):
        same = along == down
        ahead = jnp.where(same & (lane < sub), one, none)
        behind = jnp.where(same & (sub < lane), one, none)
        rank_down = jnp.sum(jnp.where(along < down, one, ahead), axis=1, keepdims=True)
        rank_along = jnp.sum(jnp.where(down < along, one, behind), axis=0, keepdims=True)
        follows = jnp.max(ahead, axis=1, keepdims=True)
        wide = jnp.broadcast_to(rank_down, (CAP, CAP))
        last_along = jnp.max(jnp.where(same, wide, none), axis=0, keepdims=True)
        last_down = jnp.max(
            jnp.where(same, jnp.broadcast_to(rank_along, (CAP, CAP)), none), axis=1, keepdims=True
        )
        return wide, jnp.broadcast_to(follows, (CAP, CAP)), last_along, jnp.broadcast_to(last_down, (CAP, CAP))

    row_along, row_down = both_ways(row_ref)
    col_along, col_down = both_ways(col_ref)
    rank_c, follows_c, last_along, last_down = sort(col_along, col_down)
    rank_r, follows_r, _, _ = sort(row_along, row_down)

    def put(place, values):
        table[pl.ds(place, 1), pl.ds(0, CAP)] = values.astype(jnp.int32)

    def in_order(rank, values):
        return jnp.sum(jnp.where(rank == lane, values, none), axis=0, keepdims=True)

    put(ORD_C, in_order(rank_c, sub))
    put(ROW_C, in_order(rank_c, row_down))
    put(KEEP_C, in_order(rank_c, follows_c))
    put(ORD_R, in_order(rank_r, sub))
    put(POS_R, in_order(rank_r, last_down))
    put(KEEP_R, in_order(rank_r, follows_r))
    ends = jnp.max(jnp.where(row_down == lane, rank_r + 1.0, none), axis=0, keepdims=True)
    put(LAST_R, jnp.where(ends == 0.0, jnp.full((1, CAP), CAP, F32), ends - 1.0))
    put(POS_K, last_along)
    put(ROW_K, row_along[:1])
    put(ALIVE, jnp.where(lane[:1] < live_ref[0, 0].astype(F32), one[:1], none[:1]))


def kernel(
    sections, index, acts, next_grad, head_grad, blocks, input_grad, block_grads,
    xc, dc, xt, dt, gu, hid, bk, wgu, wf, raw, part, hop_a, hop_b, rec_a, rec_b, rsz,
    zsum, s1, s2, acc, acc_b, ig,
    x_send, d_send, x_recv, d_recv, sh_send, ra_send, ra_hop, ra_recv, rb_send, rb_hop, rb_recv, z_send, z_recv, loc,
):
    s = lax.axis_index("section")
    t = lax.axis_index("tensor")
    y = lax.rem(t, 4)
    plane = t // 4

    def in_ring(step):
        return (s, plane * 4 + lax.rem(y + step, 4))

    across = (s, (1 - plane) * 4 + y)
    before = (lax.rem(s + sections - 1, sections), t)
    after = (lax.rem(s + 1, sections), t)

    barrier = pltpu.get_barrier_semaphore()
    for peer in (in_ring(1), in_ring(2), in_ring(3), across):
        pl.semaphore_signal(barrier, inc=1, device_id=peer, device_id_type=MESH)
    @pl.when(s < sections - 1)
    def _():
        pl.semaphore_signal(barrier, inc=1, device_id=after, device_id_type=MESH)

    blocks_in = pltpu.make_async_copy(blocks, raw, loc.at[0])
    blocks_in.start()
    own_in = pltpu.make_async_copy(acts, xc.at[0], loc.at[1])
    own_in.start()

    @pl.when(s > 0)
    def _():
        pl.semaphore_wait(barrier, 5)

    @pl.when(s == 0)
    def _():
        pl.semaphore_wait(barrier, 4)

    pending = []

    def send(src, dst, ssem, rsem, peer):
        copy = pltpu.make_async_remote_copy(
            src_ref=src, dst_ref=dst, send_sem=ssem, recv_sem=rsem, device_id=peer, device_id_type=MESH
        )
        copy.start()
        pending.append(copy)

    def arrived(dst, rsem):
        pltpu.make_async_remote_copy(
            src_ref=dst, dst_ref=dst, send_sem=rsem, recv_sem=rsem, device_id=across, device_id_type=MESH
        ).wait_recv()

    for p, cols in enumerate(PARTS):
        shift = pltpu.make_async_remote_copy(
            src_ref=next_grad.at[:, cols], dst_ref=dc.at[0, :, cols], send_sem=sh_send.at[p],
            recv_sem=d_recv.at[0, 2 * p], device_id=before, device_id_type=MESH,
        )

        @pl.when(s > 0)
        def _():
            shift.start()

        @pl.when(s == sections - 1)
        def _():
            pltpu.make_async_copy(head_grad.at[:, cols], dc.at[0, :, cols], d_recv.at[0, 2 * p]).start()

    def share_own(src, buf, ssem, rsem):
        for p, cols in enumerate(PARTS):
            send(src.at[:, cols], buf.at[4, :, cols], ssem.at[p], rsem.at[4, 2 * p], across)
            for step in (1, 3):
                send(
                    src.at[:, cols], buf.at[4 - step, :, cols], ssem.at[step + 1 + p], rsem.at[4 - step, 2 * p],
                    in_ring(step),
                )

    def round_own(buf, ssem, rsem):
        for p in (1, 0):
            for way, (place, step) in enumerate(((3, 1), (1, 3))):
                arrived(buf.at[place, :, PARTS[p]], rsem.at[place, 2 * p])
                cols = HALVES[p][way]
                send(
                    buf.at[place, :, cols], buf.at[2, :, cols], ssem.at[6 + 2 * p + way], rsem.at[2, 2 * p + way],
                    in_ring(step),
                )
        for place in (1, 3):
            cols = PARTS[1]
            send(
                buf.at[place, :, cols], buf.at[4 + place, :, cols], ssem.at[10 + place // 2], rsem.at[4 + place, 2],
                across,
            )

    def share_first(buf, ssem, rsem):
        cols = PARTS[0]
        arrived(buf.at[4, :, cols], rsem.at[4, 0])
        for step in (1, 3):
            send(
                buf.at[4, :, cols], buf.at[8 - step, :, cols], ssem.at[12 + step // 2], rsem.at[8 - step, 0],
                in_ring(step),
            )

    def cross_last(buf, ssem, rsem):
        for p in range(2):
            for way in range(2):
                arrived(buf.at[2, :, HALVES[p][way]], rsem.at[2, 2 * p + way])
        send(buf.at[2, :, PARTS[1]], buf.at[6, :, PARTS[1]], ssem.at[14], rsem.at[6, 2], across)

    def round_first(buf, ssem, rsem):
        for way, (place, step) in enumerate(((7, 1), (5, 3))):
            arrived(buf.at[place, :, PARTS[0]], rsem.at[place, 0])
            cols = HALVES[0][way]
            send(buf.at[place, :, cols], buf.at[6, :, cols], ssem.at[15 + way], rsem.at[6, way], in_ring(step))

    def rest(buf, rsem):
        for place in (4, 5, 7, 6):
            arrived(buf.at[place, :, PARTS[1]], rsem.at[place, 2])
        for way in range(2):
            arrived(buf.at[6, :, HALVES[0][way]], rsem.at[6, way])

    share_own(acts, xc, x_send, x_recv)

    blocks_in.wait()
    low = lax.broadcasted_iota(jnp.int32, (64, 128), 1) < 64
    low32 = lax.broadcasted_iota(jnp.int32, (32, 128), 1) < 64

    def prepare(g, _):
        rows = pl.ds(pl.multiple_of(g * GROUP, GROUP), GROUP)
        for i in range(SLOT // 128):
            s1[pl.ds(i * GROUP, GROUP), :] = raw[rows, pl.ds(i * 128, 128)].astype(F32)
        for j in range(GROUP):
            k = g * GROUP + j
            b = (j % 4) * 192
            for m in range(3):
                v = s1[pl.ds(m * 32 * GROUP + j, 32, stride=GROUP), :]
                turned = pltpu.roll(v, 64, 1)
                even, odd = (turned, v) if m == 1 else (v, turned)
                s2[pl.ds(b + m * 64, 32, stride=2), :] = even
                s2[pl.ds(b + m * 64 + 1, 32, stride=2), :] = odd
            both = jnp.where(low, s2[pl.ds(b, 64), :], s2[pl.ds(b + 64, 64), :])
            alive = index[ALIVE, k].astype(F32)
            both = both * alive
            down = s2[pl.ds(b + 128, 64), :] * alive
            wgu[k] = both.astype(BF16)
            wf[k, pl.ds(0, 128), pl.ds(0, 64)] = both.T.astype(BF16)
            wf[k, pl.ds(0, 128), pl.ds(64, 64)] = jnp.zeros((128, 64), BF16)
            wf[k, pl.ds(128, 64), :] = jnp.where(low, 0.0, pltpu.roll(down, 64, 1)).astype(BF16)
        return 0

    lax.fori_loop(0, CAP // GROUP // 2, prepare, 0)

    for p, cols in enumerate(PARTS):
        arrived(dc.at[0, :, cols], d_recv.at[0, 2 * p])
    share_own(dc.at[0], dc, d_send, d_recv)
    lax.fori_loop(CAP // GROUP // 2, CAP // GROUP, prepare, 0)
    bk[CAP] = jnp.zeros((64, HALF), BF16)

    def turn(buf, out, pair):
        def step(i, _):
            cols = pl.ds(pl.multiple_of(i * 128, 128), 128)
            tile = jnp.concatenate([buf[2 * pair, :, cols], buf[2 * pair + 1, :, cols]], axis=0)
            tile = tile.T
            out[2 * i, :, pl.ds(pair * 128, 128)] = tile[:64]
            out[2 * i + 1, :, pl.ds(pair * 128, 128)] = tile[64:]
            return 0

        lax.fori_loop(0, WIDTH // 128, step, 0, unroll=4)

    def forward(lanes):
        acc[...] = jnp.zeros_like(acc)

        def step(i, _):
            slots = [2 * i, 2 * i + 1]
            tokens, weights = [], []
            for j in slots:
                r = index[ROW_C, j]
                tokens += [xt[r, :, lanes], dt[r, :, lanes]]
                weights.append(wf[index[ORD_C, j]])
            none = jnp.zeros((192, 128), BF16)
            weights = jnp.concatenate(
                [jnp.concatenate([weights[0], none], axis=1), jnp.concatenate([none, weights[1]], axis=1)], axis=0
            )
            new = jnp.dot(weights, jnp.concatenate(tokens, axis=0), preferred_element_type=F32)
            total = acc[...]
            for n, j in enumerate(slots):
                total = new[n * 192:(n + 1) * 192] + index[KEEP_C, j].astype(F32) * total
                gate, upper, hg = total[:64], total[64:128], total[128:]
                sg = 0.5 + 0.5 * jnp.tanh(0.5 * gate)
                act = gate * sg
                hid[j, :, lanes] = (act * upper).astype(BF16)
                gu[j, pl.ds(0, 64), lanes] = (hg * upper * sg * (1.0 + gate * (1.0 - sg))).astype(BF16)
                gu[j, pl.ds(64, 64), lanes] = (hg * act).astype(BF16)
            acc[...] = total
            return 0

        lax.fori_loop(0, CAP // 2, step, 0, unroll=4)

    def backward(lanes, first_slot):
        acc_b[...] = jnp.zeros_like(acc_b)

        def step(i, _):
            slots = [2 * i, 2 * i + 1]
            none = jnp.zeros((64, 128), BF16)
            first, second = (wgu[index[ORD_R, j]] for j in slots)
            weights = jnp.concatenate(
                [jnp.concatenate([first, none], axis=1), jnp.concatenate([none, second], axis=1)], axis=0
            )
            both = jnp.concatenate([gu[index[POS_R, j], :, lanes] for j in slots], axis=0)
            new = jnp.dot(weights, both, preferred_element_type=F32)
            total = acc_b[...]
            for n, j in enumerate(slots):
                total = new[n * 64:(n + 1) * 64] + index[KEEP_R, j].astype(F32) * total
                bk[j] = total.astype(BF16)
            acc_b[...] = total
            return 0

        lax.fori_loop(0, CAP // 2, step, 0, unroll=4)

        def place(i, _):
            cols = pl.ds(pl.multiple_of(i * 128, 128), 128)
            both = jnp.concatenate([bk[index[LAST_R, 2 * i]], bk[index[LAST_R, 2 * i + 1]]], axis=0)
            for q in range(2):
                tile = both[:, q * 128:(q + 1) * 128].T
                part[first_slot + 2 * q, :, cols] = tile[:64]
                part[first_slot + 2 * q + 1, :, cols] = tile[64:]
            return 0

        lax.fori_loop(0, ROWS // 2, place, 0, unroll=2)

    def start_round(base, hop, rec, ssem, hsem, rsem):
        for n in range(2):
            here = pl.ds(n * WIDTH // 4, WIDTH // 4)
            up, down = QUARTERS[n], QUARTERS[2 + n]
            send(part.at[base + 2, :, up], hop.at[0, :, here], ssem.at[0, n], hsem.at[0, n], in_ring(1))
            send(part.at[base + 2, :, down], hop.at[1, :, here], ssem.at[1, n], hsem.at[1, n], in_ring(3))
            send(part.at[base + 1, :, down], rec.at[0, :, down], ssem.at[2, n], rsem.at[0, 2 + n], in_ring(1))
            send(part.at[base + 3, :, up], rec.at[1, :, up], ssem.at[3, n], rsem.at[1, n], in_ring(3))

    def add_round(base, n, hop, rec, ssem, hsem, rsem):
        here = pl.ds(n * WIDTH // 4, WIDTH // 4)
        for way, (place, step, q) in enumerate(((1, 1, n), (3, 3, 2 + n))):
            cols = QUARTERS[q]
            arrived(hop.at[way, :, here], hsem.at[way, n])
            part[base + place, :, cols] = (
                part[base + place, :, cols].astype(F32) + hop[way, :, here].astype(F32)
            ).astype(BF16)
            send(part.at[base + place, :, cols], rec.at[way, :, cols], ssem.at[4 + way, n], rsem.at[way, q], in_ring(step))

    own_in.wait()
    round_own(xc, x_send, x_recv)
    share_first(xc, x_send, x_recv)
    turn(xc, xt, 0)
    round_own(dc, d_send, d_recv)
    share_first(dc, d_send, d_recv)
    turn(dc, dt, 0)
    cross_last(xc, x_send, x_recv)
    turn(xc, xt, 1)
    cross_last(dc, d_send, d_recv)
    turn(dc, dt, 1)
    forward(pl.ds(0, HALF))
    round_first(xc, x_send, x_recv)
    round_first(dc, d_send, d_recv)
    backward(pl.ds(0, HALF), 0)
    start_round(0, hop_a, rec_a, ra_send, ra_hop, ra_recv)

    rest(xc, x_recv)
    turn(xc, xt, 2)
    turn(xc, xt, 3)
    add_round(0, 0, hop_a, rec_a, ra_send, ra_hop, ra_recv)
    rest(dc, d_recv)
    turn(dc, dt, 2)
    add_round(0, 1, hop_a, rec_a, ra_send, ra_hop, ra_recv)
    turn(dc, dt, 3)
    forward(pl.ds(HALF, HALF))
    backward(pl.ds(HALF, HALF), 4)
    start_round(4, hop_b, rec_b, rb_send, rb_hop, rb_recv)

    def grads(g, _):
        for j in range(GROUP):
            k = g * GROUP + j
            p, r = index[POS_K, k], index[ROW_K, k]
            alive = index[ALIVE, k].astype(F32)
            turned = (((1,), (1,)), ((), ()))
            d_both = lax.dot_general(xt[r], gu[p], turned, preferred_element_type=F32)
            d_down = lax.dot_general(hid[p], dt[r], turned, preferred_element_type=F32)
            b = (j % 4) * 192
            s2[pl.ds(b, 64), :] = d_both * alive
            s2[pl.ds(b + 64, 64), pl.ds(0, 64)] = d_down * alive
            even, odd = s2[pl.ds(b, 32, stride=2), :], s2[pl.ds(b + 1, 32, stride=2), :]
            d_even, d_odd = s2[pl.ds(b + 64, 32, stride=2), :], s2[pl.ds(b + 65, 32, stride=2), :]
            s1[pl.ds(j, 32, stride=GROUP), :] = jnp.where(low32, even, pltpu.roll(odd, 64, 1))
            s1[pl.ds(32 * GROUP + j, 32, stride=GROUP), :] = jnp.where(low32, pltpu.roll(even, 64, 1), odd)
            s1[pl.ds(64 * GROUP + j, 32, stride=GROUP), :] = jnp.where(low32, d_even, pltpu.roll(d_odd, 64, 1))
        rows = pl.ds(pl.multiple_of(g * GROUP, GROUP), GROUP)
        for i in range(SLOT // 128):
            raw[rows, pl.ds(i * 128, 128)] = s1[pl.ds(i * GROUP, GROUP), :].astype(BF16)
        return 0

    lax.fori_loop(0, 2, grads, 0)
    add_round(4, 0, hop_b, rec_b, rb_send, rb_hop, rb_recv)
    lax.fori_loop(2, 4, grads, 0)
    add_round(4, 1, hop_b, rec_b, rb_send, rb_hop, rb_recv)
    lax.fori_loop(4, CAP // GROUP, grads, 0)
    blocks_out = pltpu.make_async_copy(raw, block_grads, loc.at[2])
    blocks_out.start()

    for q in (0, 2, 1, 3):
        cols = QUARTERS[q]
        for n in range(2):
            arrived(rec_b.at[n, :, cols], rb_recv.at[n, q])
        zsum[:, cols] = (
            part[4, :, cols].astype(F32) + rec_b[0, :, cols].astype(F32) + rec_b[1, :, cols].astype(F32)
        ).astype(BF16)
        send(zsum.at[:, cols], rsz.at[:, cols], z_send.at[q], z_recv.at[q], across)
    outs = []
    for q in (0, 2, 1, 3):
        cols = QUARTERS[q]
        for n in range(2):
            arrived(rec_a.at[n, :, cols], ra_recv.at[n, q])
        total = part[0, :, cols].astype(F32) + rec_a[0, :, cols].astype(F32) + rec_a[1, :, cols].astype(F32)
        arrived(rsz.at[:, cols], z_recv.at[q])
        total = total + rsz[:, cols].astype(F32)
        ig[:, cols] = (dc[0, :, cols].astype(F32) + total).astype(BF16)
        copy = pltpu.make_async_copy(ig.at[:, cols], input_grad.at[:, cols], loc.at[3 + q])
        copy.start()
        outs.append(copy)

    for copy in pending:
        copy.wait_send()
    for p, cols in enumerate(PARTS):
        @pl.when(s > 0)
        def _():
            pltpu.make_async_remote_copy(
                src_ref=next_grad.at[:, cols], dst_ref=dc.at[0, :, cols], send_sem=sh_send.at[p],
                recv_sem=d_recv.at[0, 2 * p], device_id=before, device_id_type=MESH,
            ).wait_send()
    blocks_out.wait()
    for copy in outs:
        copy.wait()


def per_device(sections, acts, next_grad, head_grad, blocks, block_row, block_col, live):
    index = pl.pallas_call(
        fill_table,
        out_shape=jax.ShapeDtypeStruct((16, 128), jnp.int32),
        in_specs=[pl.BlockSpec(memory_space=pltpu.SMEM)] + [pl.BlockSpec(memory_space=pltpu.VMEM)] * 2,
        out_specs=pl.BlockSpec(memory_space=pltpu.VMEM),
    )(live, block_row, block_col)
    dma = pltpu.SemaphoreType.DMA
    any_space = pl.BlockSpec(memory_space=pl.ANY)
    input_grad, block_grads = pl.pallas_call(
        functools.partial(kernel, sections),
        out_shape=(
            jax.ShapeDtypeStruct((TOK, WIDTH), BF16),
            jax.ShapeDtypeStruct((CAP, SLOT), BF16),
        ),
        in_specs=[pl.BlockSpec(memory_space=pltpu.SMEM)] + [any_space] * 4,
        out_specs=(any_space, any_space),
        scratch_shapes=[
            pltpu.VMEM((8, TOK, WIDTH), BF16),
            pltpu.VMEM((8, TOK, WIDTH), BF16),
            pltpu.VMEM((ROWS, 64, 2 * HALF), BF16),
            pltpu.VMEM((ROWS, 64, 2 * HALF), BF16),
            pltpu.VMEM((CAP, 128, 2 * HALF), BF16),
            pltpu.VMEM((CAP, 64, 2 * HALF), BF16),
            pltpu.VMEM((CAP + 1, 64, HALF), BF16),
            pltpu.VMEM((CAP, 64, 128), BF16),
            pltpu.VMEM((CAP, 192, 128), BF16),
            pltpu.VMEM((CAP, SLOT), BF16),
            pltpu.VMEM((8, TOK, WIDTH), BF16),
            pltpu.VMEM((2, TOK, WIDTH // 2), BF16),
            pltpu.VMEM((2, TOK, WIDTH // 2), BF16),
            pltpu.VMEM((2, TOK, WIDTH), BF16),
            pltpu.VMEM((2, TOK, WIDTH), BF16),
            pltpu.VMEM((TOK, WIDTH), BF16),
            pltpu.VMEM((TOK, WIDTH), BF16),
            pltpu.VMEM((SLOT // 128 * GROUP, 128), F32),
            pltpu.VMEM((4 * 192, 128), F32),
            pltpu.VMEM((192, HALF), F32),
            pltpu.VMEM((64, HALF), F32),
            pltpu.VMEM((TOK, WIDTH), BF16),
            dma((17,)),
            dma((17,)),
            dma((8, 4)),
            dma((8, 4)),
            dma((2,)),
            dma((6, 2)),
            dma((2, 2)),
            dma((2, 4)),
            dma((6, 2)),
            dma((2, 2)),
            dma((2, 4)),
            dma((4,)),
            dma((4,)),
            dma((7,)),
        ],
        compiler_params=pltpu.CompilerParams(
            collective_id=0, has_side_effects=True, vmem_limit_bytes=63 * 2**20
        ),
    )(index, acts[0], next_grad[0], head_grad, blocks[0])
    return input_grad[None], block_grads[None]


def solution(mesh):
    return jax.shard_map(
        functools.partial(per_device, mesh.shape["section"]),
        mesh=mesh,
        in_specs=(
            P("section", "tensor", None),
            P("section", "tensor", None),
            P("tensor", None),
            P("section", "tensor", None),
            P("section", "tensor"),
            P("section", "tensor"),
            P("section", "tensor"),
        ),
        out_specs=(P("section", "tensor", None), P("section", "tensor", None)),
        check_vma=False,
    )
```

```python
import functools

import jax
import jax.numpy as jnp
from jax import lax
from jax.experimental import pallas as pl
from jax.experimental.pallas import tpu as pltpu
from jax.sharding import PartitionSpec as P

MESH = pl.DeviceIdType.MESH
BF16 = jnp.bfloat16
F32 = jnp.float32

CAP = 96
ROWS = 64
WIDTH = 4096
TOK = 64
HALF = 256
SLOT = 12288
GROUP = 16
SPLIT = 2048
REST = WIDTH - SPLIT

PARTS = (pl.ds(0, SPLIT), pl.ds(SPLIT, REST))
HALVES = (
    (pl.ds(0, SPLIT // 2), pl.ds(SPLIT // 2, SPLIT // 2)),
    (pl.ds(SPLIT, REST // 2), pl.ds(SPLIT + REST // 2, REST // 2)),
)

ORD_C, ROW_C, KEEP_C, ORD_R, POS_R, KEEP_R, LAST_R, POS_K, ROW_K, ALIVE = range(10)
PIECES_A, PIECES_B = 2, 4


def fill_table(live_ref, row_ref, col_ref, table):
    table[...] = jnp.zeros_like(table)
    lane = lax.broadcasted_iota(jnp.int32, (CAP, CAP), 1).astype(F32)
    sub = lax.broadcasted_iota(jnp.int32, (CAP, CAP), 0).astype(F32)
    one, none = jnp.ones((CAP, CAP), F32), jnp.zeros((CAP, CAP), F32)

    def both_ways(ref):
        along = jnp.broadcast_to(ref[...].astype(F32), (CAP, CAP))
        down = jnp.sum(jnp.where(lane == sub, along, none), axis=1, keepdims=True)
        return along, jnp.broadcast_to(down, (CAP, CAP))

    def sort(along, down):
        same = along == down
        ahead = jnp.where(same & (lane < sub), one, none)
        behind = jnp.where(same & (sub < lane), one, none)
        rank_down = jnp.sum(jnp.where(along < down, one, ahead), axis=1, keepdims=True)
        rank_along = jnp.sum(jnp.where(down < along, one, behind), axis=0, keepdims=True)
        follows = jnp.max(ahead, axis=1, keepdims=True)
        wide = jnp.broadcast_to(rank_down, (CAP, CAP))
        last_along = jnp.max(jnp.where(same, wide, none), axis=0, keepdims=True)
        last_down = jnp.max(
            jnp.where(same, jnp.broadcast_to(rank_along, (CAP, CAP)), none), axis=1, keepdims=True
        )
        return wide, jnp.broadcast_to(follows, (CAP, CAP)), last_along, jnp.broadcast_to(last_down, (CAP, CAP))

    row_along, row_down = both_ways(row_ref)
    col_along, col_down = both_ways(col_ref)
    rank_c, follows_c, last_along, last_down = sort(col_along, col_down)
    rank_r, follows_r, _, _ = sort(row_along, row_down)

    def put(place, values):
        table[pl.ds(place, 1), pl.ds(0, CAP)] = values.astype(jnp.int32)

    def in_order(rank, values):
        return jnp.sum(jnp.where(rank == lane, values, none), axis=0, keepdims=True)

    put(ORD_C, in_order(rank_c, sub))
    put(ROW_C, in_order(rank_c, row_down))
    put(KEEP_C, in_order(rank_c, follows_c))
    put(ORD_R, in_order(rank_r, sub))
    put(POS_R, in_order(rank_r, last_down))
    put(KEEP_R, in_order(rank_r, follows_r))
    ends = jnp.max(jnp.where(row_down == lane, rank_r + 1.0, none), axis=0, keepdims=True)
    put(LAST_R, jnp.where(ends == 0.0, jnp.full((1, CAP), CAP, F32), ends - 1.0))
    put(POS_K, last_along)
    put(ROW_K, row_along[:1])
    put(ALIVE, jnp.where(lane[:1] < live_ref[0, 0].astype(F32), one[:1], none[:1]))


def kernel(
    sections, index, acts, next_grad, head_grad, blocks, input_grad, block_grads,
    xc, dc, xt, dt, gu, hid, bk, wgu, wf, raw, part, hop_a, hop_b, rec_a, rec_b, rsz,
    zsum, s1, s2, acc, acc_b, ig,
    x_send, d_send, x_recv, d_recv, sh_send, ra_send, ra_hop, ra_recv, rb_send, rb_hop, rb_recv, z_send, z_recv, loc,
):
    s = lax.axis_index("section")
    t = lax.axis_index("tensor")
    y = lax.rem(t, 4)
    plane = t // 4

    def in_ring(step):
        return (s, plane * 4 + lax.rem(y + step, 4))

    across = (s, (1 - plane) * 4 + y)
    before = (lax.rem(s + sections - 1, sections), t)
    after = (lax.rem(s + 1, sections), t)

    barrier = pltpu.get_barrier_semaphore()
    for peer in (in_ring(1), in_ring(2), in_ring(3), across):
        pl.semaphore_signal(barrier, inc=1, device_id=peer, device_id_type=MESH)
    @pl.when(s < sections - 1)
    def _():
        pl.semaphore_signal(barrier, inc=1, device_id=after, device_id_type=MESH)

    blocks_in = pltpu.make_async_copy(blocks, raw, loc.at[0])
    blocks_in.start()
    own_in = pltpu.make_async_copy(acts, xc.at[0], loc.at[1])
    own_in.start()

    @pl.when(s > 0)
    def _():
        pl.semaphore_wait(barrier, 5)

    @pl.when(s == 0)
    def _():
        pl.semaphore_wait(barrier, 4)

    pending = []

    def send(src, dst, ssem, rsem, peer):
        copy = pltpu.make_async_remote_copy(
            src_ref=src, dst_ref=dst, send_sem=ssem, recv_sem=rsem, device_id=peer, device_id_type=MESH
        )
        copy.start()
        pending.append(copy)

    def arrived(dst, rsem):
        pltpu.make_async_remote_copy(
            src_ref=dst, dst_ref=dst, send_sem=rsem, recv_sem=rsem, device_id=across, device_id_type=MESH
        ).wait_recv()

    for p, cols in enumerate(PARTS):
        shift = pltpu.make_async_remote_copy(
            src_ref=next_grad.at[:, cols], dst_ref=dc.at[0, :, cols], send_sem=sh_send.at[p],
            recv_sem=d_recv.at[0, 2 * p], device_id=before, device_id_type=MESH,
        )

        @pl.when(s > 0)
        def _():
            shift.start()

        @pl.when(s == sections - 1)
        def _():
            pltpu.make_async_copy(head_grad.at[:, cols], dc.at[0, :, cols], d_recv.at[0, 2 * p]).start()

    def share_own(src, buf, ssem, rsem):
        for p, cols in enumerate(PARTS):
            send(src.at[:, cols], buf.at[4, :, cols], ssem.at[p], rsem.at[4, 2 * p], across)
            for step in (1, 3):
                send(
                    src.at[:, cols], buf.at[4 - step, :, cols], ssem.at[step + 1 + p], rsem.at[4 - step, 2 * p],
                    in_ring(step),
                )

    def round_own(buf, ssem, rsem):
        for p in (1, 0):
            for way, (place, step) in enumerate(((3, 1), (1, 3))):
                arrived(buf.at[place, :, PARTS[p]], rsem.at[place, 2 * p])
                cols = HALVES[p][way]
                send(
                    buf.at[place, :, cols], buf.at[2, :, cols], ssem.at[6 + 2 * p + way], rsem.at[2, 2 * p + way],
                    in_ring(step),
                )
        for place in (1, 3):
            cols = PARTS[1]
            send(
                buf.at[place, :, cols], buf.at[4 + place, :, cols], ssem.at[10 + place // 2], rsem.at[4 + place, 2],
                across,
            )

    def share_first(buf, ssem, rsem):
        cols = PARTS[0]
        arrived(buf.at[4, :, cols], rsem.at[4, 0])
        for step in (1, 3):
            send(
                buf.at[4, :, cols], buf.at[8 - step, :, cols], ssem.at[12 + step // 2], rsem.at[8 - step, 0],
                in_ring(step),
            )

    def cross_last(buf, ssem, rsem):
        for p in range(2):
            for way in range(2):
                arrived(buf.at[2, :, HALVES[p][way]], rsem.at[2, 2 * p + way])
        send(buf.at[2, :, PARTS[1]], buf.at[6, :, PARTS[1]], ssem.at[14], rsem.at[6, 2], across)

    def round_first(buf, ssem, rsem):
        for way, (place, step) in enumerate(((7, 1), (5, 3))):
            arrived(buf.at[place, :, PARTS[0]], rsem.at[place, 0])
            cols = HALVES[0][way]
            send(buf.at[place, :, cols], buf.at[6, :, cols], ssem.at[15 + way], rsem.at[6, way], in_ring(step))

    def rest_near(buf, rsem):
        for place in (5, 7):
            arrived(buf.at[place, :, PARTS[1]], rsem.at[place, 2])

    def rest_far(buf, rsem):
        for place in (4, 6):
            arrived(buf.at[place, :, PARTS[1]], rsem.at[place, 2])
        for way in range(2):
            arrived(buf.at[6, :, HALVES[0][way]], rsem.at[6, way])

    share_own(acts, xc, x_send, x_recv)

    blocks_in.wait()
    low = lax.broadcasted_iota(jnp.int32, (64, 128), 1) < 64
    low32 = lax.broadcasted_iota(jnp.int32, (32, 128), 1) < 64

    def prepare(g, _):
        rows = pl.ds(pl.multiple_of(g * GROUP, GROUP), GROUP)
        for i in range(SLOT // 128):
            s1[pl.ds(i * GROUP, GROUP), :] = raw[rows, pl.ds(i * 128, 128)].astype(F32)
        for j in range(GROUP):
            k = g * GROUP + j
            b = (j % 4) * 192
            for m in range(3):
                v = s1[pl.ds(m * 32 * GROUP + j, 32, stride=GROUP), :]
                turned = pltpu.roll(v, 64, 1)
                even, odd = (turned, v) if m == 1 else (v, turned)
                s2[pl.ds(b + m * 64, 32, stride=2), :] = even
                s2[pl.ds(b + m * 64 + 1, 32, stride=2), :] = odd
            both = jnp.where(low, s2[pl.ds(b, 64), :], s2[pl.ds(b + 64, 64), :])
            alive = index[ALIVE, k].astype(F32)
            both = both * alive
            down = s2[pl.ds(b + 128, 64), :] * alive
            wgu[k] = both.astype(BF16)
            wf[k, pl.ds(0, 128), pl.ds(0, 64)] = both.T.astype(BF16)
            wf[k, pl.ds(0, 128), pl.ds(64, 64)] = jnp.zeros((128, 64), BF16)
            wf[k, pl.ds(128, 64), :] = jnp.where(low, 0.0, pltpu.roll(down, 64, 1)).astype(BF16)
        return 0

    lax.fori_loop(0, CAP // GROUP // 2, prepare, 0)

    for p, cols in enumerate(PARTS):
        arrived(dc.at[0, :, cols], d_recv.at[0, 2 * p])
    share_own(dc.at[0], dc, d_send, d_recv)
    lax.fori_loop(CAP // GROUP // 2, CAP // GROUP, prepare, 0)
    bk[CAP] = jnp.zeros((64, HALF), BF16)

    def turn(buf, out, pair, first, second):
        def step(i, _):
            cols = pl.ds(pl.multiple_of(i * 128, 128), 128)
            tile = jnp.concatenate([buf[first, :, cols], buf[second, :, cols]], axis=0)
            tile = tile.T
            out[2 * i, :, pl.ds(pair * 128, 128)] = tile[:64]
            out[2 * i + 1, :, pl.ds(pair * 128, 128)] = tile[64:]
            return 0

        lax.fori_loop(0, WIDTH // 128, step, 0, unroll=4)

    def forward(start, width):
        lanes, here = pl.ds(start, width), pl.ds(0, width)
        acc[...] = jnp.zeros_like(acc)

        def step(i, _):
            slots = [2 * i, 2 * i + 1]
            tokens, weights = [], []
            for j in slots:
                r = index[ROW_C, j]
                tokens += [xt[r, :, lanes], dt[r, :, lanes]]
                weights.append(wf[index[ORD_C, j]])
            none = jnp.zeros((192, 128), BF16)
            weights = jnp.concatenate(
                [jnp.concatenate([weights[0], none], axis=1), jnp.concatenate([none, weights[1]], axis=1)], axis=0
            )
            new = jnp.dot(weights, jnp.concatenate(tokens, axis=0), preferred_element_type=F32)
            total = acc[:, here]
            for n, j in enumerate(slots):
                total = new[n * 192:(n + 1) * 192] + index[KEEP_C, j].astype(F32) * total
                gate, upper, hg = total[:64], total[64:128], total[128:]
                sg = 0.5 + 0.5 * jnp.tanh(0.5 * gate)
                act = gate * sg
                hid[j, :, lanes] = (act * upper).astype(BF16)
                gu[j, pl.ds(0, 64), lanes] = (hg * upper * sg * (1.0 + gate * (1.0 - sg))).astype(BF16)
                gu[j, pl.ds(64, 64), lanes] = (hg * act).astype(BF16)
            acc[:, here] = total
            return 0

        lax.fori_loop(0, CAP // 2, step, 0, unroll=4)

    def backward(start, width, pairs):
        lanes, here = pl.ds(start, width), pl.ds(0, width)
        acc_b[...] = jnp.zeros_like(acc_b)

        def step(i, _):
            slots = [2 * i, 2 * i + 1]
            none = jnp.zeros((64, 128), BF16)
            first, second = (wgu[index[ORD_R, j]] for j in slots)
            weights = jnp.concatenate(
                [jnp.concatenate([first, none], axis=1), jnp.concatenate([none, second], axis=1)], axis=0
            )
            both = jnp.concatenate([gu[index[POS_R, j], :, lanes] for j in slots], axis=0)
            new = jnp.dot(weights, both, preferred_element_type=F32)
            total = acc_b[:, here]
            for n, j in enumerate(slots):
                total = new[n * 64:(n + 1) * 64] + index[KEEP_R, j].astype(F32) * total
                bk[j, :, here] = total.astype(BF16)
            acc_b[:, here] = total
            return 0

        lax.fori_loop(0, CAP // 2, step, 0, unroll=4)

        def place(i, _):
            cols = pl.ds(pl.multiple_of(i * 128, 128), 128)
            both = jnp.concatenate(
                [bk[index[LAST_R, 2 * i], :, here], bk[index[LAST_R, 2 * i + 1], :, here]], axis=0
            )
            for q, (first, second) in enumerate(pairs):
                tile = both[:, q * 128:(q + 1) * 128].T
                part[first, :, cols] = tile[:64]
                part[second, :, cols] = tile[64:]
            return 0

        lax.fori_loop(0, ROWS // 2, place, 0, unroll=2)

    def piece(half, n, pieces):
        return pl.ds(half * WIDTH // 2 + n * (WIDTH // 2 // pieces), WIDTH // 2 // pieces)

    def start_far(base, pieces, hop, ssem, hsem):
        for n in range(pieces):
            for way, step in enumerate((1, 3)):
                send(
                    part.at[base + 2, :, piece(way, n, pieces)], hop.at[way, :, piece(0, n, pieces)],
                    ssem.at[way, n], hsem.at[way, n], in_ring(step),
                )

    def start_near(base, pieces, rec, ssem, rsem):
        for n in range(pieces):
            for way, step in enumerate((1, 3)):
                cols = piece(1 - way, n, pieces)
                send(
                    part.at[base + step, :, cols], rec.at[way, :, cols], ssem.at[2 + way, n],
                    rsem.at[way, 1 - way, n], in_ring(step),
                )

    def add_round(base, n, pieces, hop, rec, ssem, hsem, rsem):
        here = piece(0, n, pieces)
        for way, step in enumerate((1, 3)):
            cols = piece(way, n, pieces)
            arrived(hop.at[way, :, here], hsem.at[way, n])
            part[base + step, :, cols] = (
                part[base + step, :, cols].astype(F32) + hop[way, :, here].astype(F32)
            ).astype(BF16)
            send(part.at[base + step, :, cols], rec.at[way, :, cols], ssem.at[4 + way, n], rsem.at[way, way, n], in_ring(step))

    def collected(half, n, pieces, rec, rsem):
        for way in range(2):
            arrived(rec.at[way, :, piece(half, n, pieces)], rsem.at[way, half, n])

    own_in.wait()
    round_own(xc, x_send, x_recv)
    share_first(xc, x_send, x_recv)
    turn(xc, xt, 0, 0, 1)
    round_own(dc, d_send, d_recv)
    share_first(dc, d_send, d_recv)
    turn(dc, dt, 0, 0, 1)
    cross_last(xc, x_send, x_recv)
    turn(xc, xt, 1, 2, 3)
    cross_last(dc, d_send, d_recv)
    turn(dc, dt, 1, 2, 3)
    forward(0, HALF)
    round_first(xc, x_send, x_recv)
    round_first(dc, d_send, d_recv)
    backward(0, HALF, ((0, 1), (2, 3)))
    start_far(0, PIECES_A, hop_a, ra_send, ra_hop)
    start_near(0, PIECES_A, rec_a, ra_send, ra_recv)

    rest_near(xc, x_recv)
    turn(xc, xt, 2, 5, 7)
    rest_near(dc, d_recv)
    turn(dc, dt, 2, 5, 7)
    forward(HALF, HALF // 2)
    add_round(0, 0, PIECES_A, hop_a, rec_a, ra_send, ra_hop, ra_recv)
    backward(HALF, HALF // 2, ((5, 7),))
    start_near(4, PIECES_B, rec_b, rb_send, rb_recv)
    add_round(0, 1, PIECES_A, hop_a, rec_a, ra_send, ra_hop, ra_recv)
    rest_far(xc, x_recv)
    turn(xc, xt, 3, 4, 6)
    rest_far(dc, d_recv)
    turn(dc, dt, 3, 4, 6)
    forward(HALF + HALF // 2, HALF // 2)
    backward(HALF + HALF // 2, HALF // 2, ((4, 6),))
    start_far(4, PIECES_B, hop_b, rb_send, rb_hop)

    def grads(g, _):
        for j in range(GROUP):
            k = g * GROUP + j
            p, r = index[POS_K, k], index[ROW_K, k]
            alive = index[ALIVE, k].astype(F32)
            turned = (((1,), (1,)), ((), ()))
            d_both = lax.dot_general(xt[r], gu[p], turned, preferred_element_type=F32)
            d_down = lax.dot_general(hid[p], dt[r], turned, preferred_element_type=F32)
            b = (j % 4) * 192
            s2[pl.ds(b, 64), :] = d_both * alive
            s2[pl.ds(b + 64, 64), pl.ds(0, 64)] = d_down * alive
            even, odd = s2[pl.ds(b, 32, stride=2), :], s2[pl.ds(b + 1, 32, stride=2), :]
            d_even, d_odd = s2[pl.ds(b + 64, 32, stride=2), :], s2[pl.ds(b + 65, 32, stride=2), :]
            s1[pl.ds(j, 32, stride=GROUP), :] = jnp.where(low32, even, pltpu.roll(odd, 64, 1))
            s1[pl.ds(32 * GROUP + j, 32, stride=GROUP), :] = jnp.where(low32, pltpu.roll(even, 64, 1), odd)
            s1[pl.ds(64 * GROUP + j, 32, stride=GROUP), :] = jnp.where(low32, d_even, pltpu.roll(d_odd, 64, 1))
        rows = pl.ds(pl.multiple_of(g * GROUP, GROUP), GROUP)
        for i in range(SLOT // 128):
            raw[rows, pl.ds(i * 128, 128)] = s1[pl.ds(i * GROUP, GROUP), :].astype(BF16)
        return 0

    def cross_sum(n):
        for half in range(2):
            cols = piece(half, n, PIECES_B)
            collected(half, n, PIECES_B, rec_b, rb_recv)
            zsum[:, cols] = (
                part[4, :, cols].astype(F32) + rec_b[0, :, cols].astype(F32) + rec_b[1, :, cols].astype(F32)
            ).astype(BF16)
            send(zsum.at[:, cols], rsz.at[:, cols], z_send.at[half, n], z_recv.at[half, n], across)

    for n in range(PIECES_B):
        lax.fori_loop(n, n + 1, grads, 0)
        add_round(4, n, PIECES_B, hop_b, rec_b, rb_send, rb_hop, rb_recv)
    cross_sum(0)
    lax.fori_loop(4, 5, grads, 0)
    cross_sum(1)
    lax.fori_loop(5, 6, grads, 0)
    blocks_out = pltpu.make_async_copy(raw, block_grads, loc.at[2])
    blocks_out.start()
    cross_sum(2)
    cross_sum(3)
    for n in range(PIECES_A):
        for half in range(2):
            collected(half, n, PIECES_A, rec_a, ra_recv)
    outs = []
    for n in range(PIECES_B):
        for half in range(2):
            cols = piece(half, n, PIECES_B)
            total = part[0, :, cols].astype(F32) + rec_a[0, :, cols].astype(F32) + rec_a[1, :, cols].astype(F32)
            arrived(rsz.at[:, cols], z_recv.at[half, n])
            total = total + rsz[:, cols].astype(F32)
            ig[:, cols] = (dc[0, :, cols].astype(F32) + total).astype(BF16)
            copy = pltpu.make_async_copy(ig.at[:, cols], input_grad.at[:, cols], loc.at[3 + 2 * n + half])
            copy.start()
            outs.append(copy)

    for copy in pending:
        copy.wait_send()
    for p, cols in enumerate(PARTS):
        @pl.when(s > 0)
        def _():
            pltpu.make_async_remote_copy(
                src_ref=next_grad.at[:, cols], dst_ref=dc.at[0, :, cols], send_sem=sh_send.at[p],
                recv_sem=d_recv.at[0, 2 * p], device_id=before, device_id_type=MESH,
            ).wait_send()
    blocks_out.wait()
    for copy in outs:
        copy.wait()


def copy_kernel(a, b, a_out, b_out, a_buf, b_buf, sems):
    pairs = [(a, a_buf, a_out, pl.ds(0, TOK))]
    for n in range(CAP // GROUP):
        pairs.append((b, b_buf, b_out, pl.ds(n * GROUP, GROUP)))
    ins = [pltpu.make_async_copy(src.at[r], buf.at[r], sems.at[0, n]) for n, (src, buf, _, r) in enumerate(pairs)]
    outs = [pltpu.make_async_copy(buf.at[r], dst.at[r], sems.at[1, n]) for n, (_, buf, dst, r) in enumerate(pairs)]
    for copy in ins:
        copy.start()
    for into, out in zip(ins, outs):
        into.wait()
        out.start()
    for copy in outs:
        copy.wait()


def hand_over(input_grad, block_grads):
    any_space = pl.BlockSpec(memory_space=pl.ANY)
    input_grad, block_grads = pl.pallas_call(
        copy_kernel,
        out_shape=(
            jax.ShapeDtypeStruct(input_grad.shape, BF16),
            jax.ShapeDtypeStruct(block_grads.shape, BF16),
        ),
        in_specs=[any_space] * 2,
        out_specs=(any_space, any_space),
        scratch_shapes=[
            pltpu.VMEM(input_grad.shape, BF16),
            pltpu.VMEM(block_grads.shape, BF16),
            pltpu.SemaphoreType.DMA((2, 1 + CAP // GROUP)),
        ],
        compiler_params=pltpu.CompilerParams(vmem_limit_bytes=60 * 2**20),
    )(input_grad, block_grads)
    return input_grad[None], block_grads[None]


def per_device(sections, acts, next_grad, head_grad, blocks, block_row, block_col, live):
    index = pl.pallas_call(
        fill_table,
        out_shape=jax.ShapeDtypeStruct((16, 128), jnp.int32),
        in_specs=[pl.BlockSpec(memory_space=pltpu.SMEM)] + [pl.BlockSpec(memory_space=pltpu.VMEM)] * 2,
        out_specs=pl.BlockSpec(memory_space=pltpu.VMEM),
    )(live, block_row, block_col)
    dma = pltpu.SemaphoreType.DMA
    any_space = pl.BlockSpec(memory_space=pl.ANY)
    input_grad, block_grads = pl.pallas_call(
        functools.partial(kernel, sections),
        out_shape=(
            jax.ShapeDtypeStruct((TOK, WIDTH), BF16),
            jax.ShapeDtypeStruct((CAP, SLOT), BF16),
        ),
        in_specs=[pl.BlockSpec(memory_space=pltpu.SMEM)] + [any_space] * 4,
        out_specs=(any_space, any_space),
        scratch_shapes=[
            pltpu.VMEM((8, TOK, WIDTH), BF16),
            pltpu.VMEM((8, TOK, WIDTH), BF16),
            pltpu.VMEM((ROWS, 64, 2 * HALF), BF16),
            pltpu.VMEM((ROWS, 64, 2 * HALF), BF16),
            pltpu.VMEM((CAP, 128, 2 * HALF), BF16),
            pltpu.VMEM((CAP, 64, 2 * HALF), BF16),
            pltpu.VMEM((CAP + 1, 64, HALF), BF16),
            pltpu.VMEM((CAP, 64, 128), BF16),
            pltpu.VMEM((CAP, 192, 128), BF16),
            pltpu.VMEM((CAP, SLOT), BF16),
            pltpu.VMEM((8, TOK, WIDTH), BF16),
            pltpu.VMEM((2, TOK, WIDTH // 2), BF16),
            pltpu.VMEM((2, TOK, WIDTH // 2), BF16),
            pltpu.VMEM((2, TOK, WIDTH), BF16),
            pltpu.VMEM((2, TOK, WIDTH), BF16),
            pltpu.VMEM((TOK, WIDTH), BF16),
            pltpu.VMEM((TOK, WIDTH), BF16),
            pltpu.VMEM((SLOT // 128 * GROUP, 128), F32),
            pltpu.VMEM((4 * 192, 128), F32),
            pltpu.VMEM((192, HALF), F32),
            pltpu.VMEM((64, HALF), F32),
            pltpu.VMEM((TOK, WIDTH), BF16),
            dma((17,)),
            dma((17,)),
            dma((8, 4)),
            dma((8, 4)),
            dma((2,)),
            dma((6, PIECES_A)),
            dma((2, PIECES_A)),
            dma((2, 2, PIECES_A)),
            dma((6, PIECES_B)),
            dma((2, PIECES_B)),
            dma((2, 2, PIECES_B)),
            dma((2, PIECES_B)),
            dma((2, PIECES_B)),
            dma((3 + 2 * PIECES_B,)),
        ],
        compiler_params=pltpu.CompilerParams(
            collective_id=0, has_side_effects=True, vmem_limit_bytes=63 * 2**20
        ),
    )(index, acts[0], next_grad[0], head_grad, blocks[0])
    return hand_over(input_grad, block_grads)


def solution(mesh):
    return jax.shard_map(
        functools.partial(per_device, mesh.shape["section"]),
        mesh=mesh,
        in_specs=(
            P("section", "tensor", None),
            P("section", "tensor", None),
            P("tensor", None),
            P("section", "tensor", None),
            P("section", "tensor"),
            P("section", "tensor"),
            P("section", "tensor"),
        ),
        out_specs=(P("section", "tensor", None), P("section", "tensor", None)),
        check_vma=False,
    )
```

```python
import functools

import jax
import jax.numpy as jnp
from jax import lax
from jax.experimental import pallas as pl
from jax.experimental.pallas import tpu as pltpu
from jax.sharding import PartitionSpec as P

MESH = pl.DeviceIdType.MESH
BF16 = jnp.bfloat16
F32 = jnp.float32

CAP = 96
ROWS = 64
WIDTH = 4096
TOK = 64
HALF = 256
SLOT = 12288
GROUP = 16
SPLIT = 2048
REST = WIDTH - SPLIT

PARTS = (pl.ds(0, SPLIT), pl.ds(SPLIT, REST))
HALVES = (
    (pl.ds(0, SPLIT // 2), pl.ds(SPLIT // 2, SPLIT // 2)),
    (pl.ds(SPLIT, REST // 2), pl.ds(SPLIT + REST // 2, REST // 2)),
)

ORD_C, ROW_C, KEEP_C, ORD_R, POS_R, KEEP_R, LAST_R, POS_K, ROW_K, ALIVE = range(10)
PIECES_A, PIECES_B = 2, 4


def fill_table(live_ref, row_ref, col_ref, table):
    table[...] = jnp.zeros_like(table)
    lane = lax.broadcasted_iota(jnp.int32, (CAP, CAP), 1).astype(F32)
    sub = lax.broadcasted_iota(jnp.int32, (CAP, CAP), 0).astype(F32)
    one, none = jnp.ones((CAP, CAP), F32), jnp.zeros((CAP, CAP), F32)

    def both_ways(ref):
        along = jnp.broadcast_to(ref[...].astype(F32), (CAP, CAP))
        down = jnp.sum(jnp.where(lane == sub, along, none), axis=1, keepdims=True)
        return along, jnp.broadcast_to(down, (CAP, CAP))

    def sort(along, down):
        same = along == down
        ahead = jnp.where(same & (lane < sub), one, none)
        behind = jnp.where(same & (sub < lane), one, none)
        rank_down = jnp.sum(jnp.where(along < down, one, ahead), axis=1, keepdims=True)
        rank_along = jnp.sum(jnp.where(down < along, one, behind), axis=0, keepdims=True)
        follows = jnp.max(ahead, axis=1, keepdims=True)
        wide = jnp.broadcast_to(rank_down, (CAP, CAP))
        last_along = jnp.max(jnp.where(same, wide, none), axis=0, keepdims=True)
        last_down = jnp.max(
            jnp.where(same, jnp.broadcast_to(rank_along, (CAP, CAP)), none), axis=1, keepdims=True
        )
        return wide, jnp.broadcast_to(follows, (CAP, CAP)), last_along, jnp.broadcast_to(last_down, (CAP, CAP))

    row_along, row_down = both_ways(row_ref)
    col_along, col_down = both_ways(col_ref)
    rank_c, follows_c, last_along, last_down = sort(col_along, col_down)
    rank_r, follows_r, _, _ = sort(row_along, row_down)

    def put(place, values):
        table[pl.ds(place, 1), pl.ds(0, CAP)] = values.astype(jnp.int32)

    def in_order(rank, values):
        return jnp.sum(jnp.where(rank == lane, values, none), axis=0, keepdims=True)

    put(ORD_C, in_order(rank_c, sub))
    put(ROW_C, in_order(rank_c, row_down))
    put(KEEP_C, in_order(rank_c, follows_c))
    put(ORD_R, in_order(rank_r, sub))
    put(POS_R, in_order(rank_r, last_down))
    put(KEEP_R, in_order(rank_r, follows_r))
    ends = jnp.max(jnp.where(row_down == lane, rank_r + 1.0, none), axis=0, keepdims=True)
    put(LAST_R, jnp.where(ends == 0.0, jnp.full((1, CAP), CAP, F32), ends - 1.0))
    put(POS_K, last_along)
    put(ROW_K, row_along[:1])
    put(ALIVE, jnp.where(lane[:1] < live_ref[0, 0].astype(F32), one[:1], none[:1]))


def kernel(
    sections, index, acts, next_grad, head_grad, blocks, input_grad, block_grads,
    xc, dc, xt, dt, gu, hid, bk, wgu, wf, raw, part, hop_a, hop_b, rec_a, rec_b, rsz,
    zsum, s1, s2, acc, acc_b, ig,
    x_send, d_send, x_recv, d_recv, sh_send, ra_send, ra_hop, ra_recv, rb_send, rb_hop, rb_recv, z_send, z_recv, loc,
):
    s = lax.axis_index("section")
    t = lax.axis_index("tensor")
    y = lax.rem(t, 4)
    plane = t // 4

    def in_ring(step):
        return (s, plane * 4 + lax.rem(y + step, 4))

    across = (s, (1 - plane) * 4 + y)
    before = (lax.rem(s + sections - 1, sections), t)
    after = (lax.rem(s + 1, sections), t)

    barrier = pltpu.get_barrier_semaphore()
    for peer in (in_ring(1), in_ring(2), in_ring(3), across):
        pl.semaphore_signal(barrier, inc=1, device_id=peer, device_id_type=MESH)
    @pl.when(s < sections - 1)
    def _():
        pl.semaphore_signal(barrier, inc=1, device_id=after, device_id_type=MESH)

    blocks_in = pltpu.make_async_copy(blocks, raw, loc.at[0])
    blocks_in.start()
    own_in = pltpu.make_async_copy(acts, xc.at[0], loc.at[1])
    own_in.start()

    @pl.when(s > 0)
    def _():
        pl.semaphore_wait(barrier, 5)

    @pl.when(s == 0)
    def _():
        pl.semaphore_wait(barrier, 4)

    pending = []

    def send(src, dst, ssem, rsem, peer):
        copy = pltpu.make_async_remote_copy(
            src_ref=src, dst_ref=dst, send_sem=ssem, recv_sem=rsem, device_id=peer, device_id_type=MESH
        )
        copy.start()
        pending.append(copy)

    def arrived(dst, rsem):
        pltpu.make_async_remote_copy(
            src_ref=dst, dst_ref=dst, send_sem=rsem, recv_sem=rsem, device_id=across, device_id_type=MESH
        ).wait_recv()

    for p, cols in enumerate(PARTS):
        shift = pltpu.make_async_remote_copy(
            src_ref=next_grad.at[:, cols], dst_ref=dc.at[0, :, cols], send_sem=sh_send.at[p],
            recv_sem=d_recv.at[0, 2 * p], device_id=before, device_id_type=MESH,
        )

        @pl.when(s > 0)
        def _():
            shift.start()

        @pl.when(s == sections - 1)
        def _():
            pltpu.make_async_copy(head_grad.at[:, cols], dc.at[0, :, cols], d_recv.at[0, 2 * p]).start()

    def share_own(src, buf, ssem, rsem):
        for p, cols in enumerate(PARTS):
            send(src.at[:, cols], buf.at[4, :, cols], ssem.at[p], rsem.at[4, 2 * p], across)
            for step in (1, 3):
                send(
                    src.at[:, cols], buf.at[4 - step, :, cols], ssem.at[step + 1 + p], rsem.at[4 - step, 2 * p],
                    in_ring(step),
                )

    def round_own(buf, ssem, rsem):
        for p in (1, 0):
            for way, (place, step) in enumerate(((3, 1), (1, 3))):
                arrived(buf.at[place, :, PARTS[p]], rsem.at[place, 2 * p])
                cols = HALVES[p][way]
                send(
                    buf.at[place, :, cols], buf.at[2, :, cols], ssem.at[6 + 2 * p + way], rsem.at[2, 2 * p + way],
                    in_ring(step),
                )
        for place in (1, 3):
            cols = PARTS[1]
            send(
                buf.at[place, :, cols], buf.at[4 + place, :, cols], ssem.at[10 + place // 2], rsem.at[4 + place, 2],
                across,
            )

    def share_first(buf, ssem, rsem):
        cols = PARTS[0]
        arrived(buf.at[4, :, cols], rsem.at[4, 0])
        for step in (1, 3):
            send(
                buf.at[4, :, cols], buf.at[8 - step, :, cols], ssem.at[12 + step // 2], rsem.at[8 - step, 0],
                in_ring(step),
            )

    def cross_last(buf, ssem, rsem):
        for p in range(2):
            for way in range(2):
                arrived(buf.at[2, :, HALVES[p][way]], rsem.at[2, 2 * p + way])
        send(buf.at[2, :, PARTS[1]], buf.at[6, :, PARTS[1]], ssem.at[14], rsem.at[6, 2], across)

    def round_first(buf, ssem, rsem):
        for way, (place, step) in enumerate(((7, 1), (5, 3))):
            arrived(buf.at[place, :, PARTS[0]], rsem.at[place, 0])
            cols = HALVES[0][way]
            send(buf.at[place, :, cols], buf.at[6, :, cols], ssem.at[15 + way], rsem.at[6, way], in_ring(step))

    def rest_near(buf, rsem):
        for place in (5, 7):
            arrived(buf.at[place, :, PARTS[1]], rsem.at[place, 2])

    def rest_far(buf, rsem):
        for place in (4, 6):
            arrived(buf.at[place, :, PARTS[1]], rsem.at[place, 2])
        for way in range(2):
            arrived(buf.at[6, :, HALVES[0][way]], rsem.at[6, way])

    share_own(acts, xc, x_send, x_recv)

    blocks_in.wait()
    low = lax.broadcasted_iota(jnp.int32, (64, 128), 1) < 64
    low32 = lax.broadcasted_iota(jnp.int32, (32, 128), 1) < 64

    def prepare(g, _):
        rows = pl.ds(pl.multiple_of(g * GROUP, GROUP), GROUP)
        for i in range(SLOT // 128):
            s1[pl.ds(i * GROUP, GROUP), :] = raw[rows, pl.ds(i * 128, 128)].astype(F32)
        for j in range(GROUP):
            k = g * GROUP + j
            b = (j % 4) * 192
            for m in range(3):
                v = s1[pl.ds(m * 32 * GROUP + j, 32, stride=GROUP), :]
                turned = pltpu.roll(v, 64, 1)
                even, odd = (turned, v) if m == 1 else (v, turned)
                s2[pl.ds(b + m * 64, 32, stride=2), :] = even
                s2[pl.ds(b + m * 64 + 1, 32, stride=2), :] = odd
            both = jnp.where(low, s2[pl.ds(b, 64), :], s2[pl.ds(b + 64, 64), :])
            alive = index[ALIVE, k].astype(F32)
            both = both * alive
            down = s2[pl.ds(b + 128, 64), :] * alive
            wgu[k] = both.astype(BF16)
            wf[k, pl.ds(0, 128), pl.ds(0, 64)] = both.T.astype(BF16)
            wf[k, pl.ds(0, 128), pl.ds(64, 64)] = jnp.zeros((128, 64), BF16)
            wf[k, pl.ds(128, 64), :] = jnp.where(low, 0.0, pltpu.roll(down, 64, 1)).astype(BF16)
        return 0

    lax.fori_loop(0, CAP // GROUP // 2, prepare, 0)

    for p, cols in enumerate(PARTS):
        arrived(dc.at[0, :, cols], d_recv.at[0, 2 * p])
    share_own(dc.at[0], dc, d_send, d_recv)
    lax.fori_loop(CAP // GROUP // 2, CAP // GROUP, prepare, 0)
    bk[CAP] = jnp.zeros((64, HALF), BF16)

    def turn(buf, out, pair, first, second):
        def step(i, _):
            cols = pl.ds(pl.multiple_of(i * 128, 128), 128)
            tile = jnp.concatenate([buf[first, :, cols], buf[second, :, cols]], axis=0)
            tile = tile.T
            out[2 * i, :, pl.ds(pair * 128, 128)] = tile[:64]
            out[2 * i + 1, :, pl.ds(pair * 128, 128)] = tile[64:]
            return 0

        lax.fori_loop(0, WIDTH // 128, step, 0, unroll=4)

    def forward(start, width):
        lanes, here = pl.ds(start, width), pl.ds(0, width)
        acc[...] = jnp.zeros_like(acc)

        def step(i, _):
            slots = [2 * i, 2 * i + 1]
            tokens, weights = [], []
            for j in slots:
                r = index[ROW_C, j]
                tokens += [xt[r, :, lanes], dt[r, :, lanes]]
                weights.append(wf[index[ORD_C, j]])
            none = jnp.zeros((192, 128), BF16)
            weights = jnp.concatenate(
                [jnp.concatenate([weights[0], none], axis=1), jnp.concatenate([none, weights[1]], axis=1)], axis=0
            )
            new = jnp.dot(weights, jnp.concatenate(tokens, axis=0), preferred_element_type=F32)
            total = acc[:, here]
            for n, j in enumerate(slots):
                total = new[n * 192:(n + 1) * 192] + index[KEEP_C, j].astype(F32) * total
                gate, upper, hg = total[:64], total[64:128], total[128:]
                sg = 0.5 + 0.5 * jnp.tanh(0.5 * gate)
                act = gate * sg
                hid[j, :, lanes] = (act * upper).astype(BF16)
                gu[j, pl.ds(0, 64), lanes] = (hg * upper * sg * (1.0 + gate * (1.0 - sg))).astype(BF16)
                gu[j, pl.ds(64, 64), lanes] = (hg * act).astype(BF16)
            acc[:, here] = total
            return 0

        lax.fori_loop(0, CAP // 2, step, 0, unroll=4)

    def backward(start, width, pairs):
        lanes, here = pl.ds(start, width), pl.ds(0, width)
        acc_b[...] = jnp.zeros_like(acc_b)

        def step(i, _):
            slots = [2 * i, 2 * i + 1]
            none = jnp.zeros((64, 128), BF16)
            first, second = (wgu[index[ORD_R, j]] for j in slots)
            weights = jnp.concatenate(
                [jnp.concatenate([first, none], axis=1), jnp.concatenate([none, second], axis=1)], axis=0
            )
            both = jnp.concatenate([gu[index[POS_R, j], :, lanes] for j in slots], axis=0)
            new = jnp.dot(weights, both, preferred_element_type=F32)
            total = acc_b[:, here]
            for n, j in enumerate(slots):
                total = new[n * 64:(n + 1) * 64] + index[KEEP_R, j].astype(F32) * total
                bk[j, :, here] = total.astype(BF16)
            acc_b[:, here] = total
            return 0

        lax.fori_loop(0, CAP // 2, step, 0, unroll=4)

        def place(i, _):
            cols = pl.ds(pl.multiple_of(i * 128, 128), 128)
            both = jnp.concatenate(
                [bk[index[LAST_R, 2 * i], :, here], bk[index[LAST_R, 2 * i + 1], :, here]], axis=0
            )
            for q, (first, second) in enumerate(pairs):
                tile = both[:, q * 128:(q + 1) * 128].T
                part[first, :, cols] = tile[:64]
                part[second, :, cols] = tile[64:]
            return 0

        lax.fori_loop(0, ROWS // 2, place, 0, unroll=2)

    def piece(half, n, pieces):
        return pl.ds(half * WIDTH // 2 + n * (WIDTH // 2 // pieces), WIDTH // 2 // pieces)

    def start_far(base, pieces, hop, ssem, hsem):
        for n in range(pieces):
            for way, step in enumerate((1, 3)):
                send(
                    part.at[base + 2, :, piece(way, n, pieces)], hop.at[way, :, piece(0, n, pieces)],
                    ssem.at[way, n], hsem.at[way, n], in_ring(step),
                )

    def start_near(base, pieces, rec, ssem, rsem, first=0, end=None):
        for n in range(first, pieces if end is None else end):
            for way, step in enumerate((1, 3)):
                cols = piece(1 - way, n, pieces)
                send(
                    part.at[base + step, :, cols], rec.at[way, :, cols], ssem.at[2 + way, n],
                    rsem.at[way, 1 - way, n], in_ring(step),
                )

    def add_round(base, n, pieces, hop, rec, ssem, hsem, rsem):
        here = piece(0, n, pieces)
        for way, step in enumerate((1, 3)):
            cols = piece(way, n, pieces)
            arrived(hop.at[way, :, here], hsem.at[way, n])
            part[base + step, :, cols] = (
                part[base + step, :, cols].astype(F32) + hop[way, :, here].astype(F32)
            ).astype(BF16)
            send(part.at[base + step, :, cols], rec.at[way, :, cols], ssem.at[4 + way, n], rsem.at[way, way, n], in_ring(step))

    def collected(half, n, pieces, rec, rsem):
        for way in range(2):
            arrived(rec.at[way, :, piece(half, n, pieces)], rsem.at[way, half, n])

    own_in.wait()
    round_own(xc, x_send, x_recv)
    share_first(xc, x_send, x_recv)
    turn(xc, xt, 0, 0, 1)
    round_own(dc, d_send, d_recv)
    share_first(dc, d_send, d_recv)
    turn(dc, dt, 0, 0, 1)
    cross_last(xc, x_send, x_recv)
    turn(xc, xt, 1, 2, 3)
    cross_last(dc, d_send, d_recv)
    turn(dc, dt, 1, 2, 3)
    forward(0, HALF)
    round_first(xc, x_send, x_recv)
    backward(0, HALF, ((0, 1), (2, 3)))
    round_first(dc, d_send, d_recv)
    start_far(0, PIECES_A, hop_a, ra_send, ra_hop)
    start_near(0, PIECES_A, rec_a, ra_send, ra_recv, 0, 1)

    rest_near(xc, x_recv)
    turn(xc, xt, 2, 5, 7)
    rest_near(dc, d_recv)
    turn(dc, dt, 2, 5, 7)
    forward(HALF, HALF // 2)
    add_round(0, 0, PIECES_A, hop_a, rec_a, ra_send, ra_hop, ra_recv)
    backward(HALF, HALF // 2, ((5, 7),))
    start_near(4, PIECES_B, rec_b, rb_send, rb_recv)
    add_round(0, 1, PIECES_A, hop_a, rec_a, ra_send, ra_hop, ra_recv)
    rest_far(xc, x_recv)
    turn(xc, xt, 3, 4, 6)
    rest_far(dc, d_recv)
    turn(dc, dt, 3, 4, 6)
    forward(HALF + HALF // 2, HALF // 2)
    backward(HALF + HALF // 2, HALF // 2, ((4, 6),))
    start_far(4, PIECES_B, hop_b, rb_send, rb_hop)

    def grads(g, _):
        for j in range(GROUP):
            k = g * GROUP + j
            p, r = index[POS_K, k], index[ROW_K, k]
            alive = index[ALIVE, k].astype(F32)
            turned = (((1,), (1,)), ((), ()))
            d_both = lax.dot_general(xt[r], gu[p], turned, preferred_element_type=F32)
            d_down = lax.dot_general(hid[p], dt[r], turned, preferred_element_type=F32)
            b = (j % 4) * 192
            s2[pl.ds(b, 64), :] = d_both * alive
            s2[pl.ds(b + 64, 64), pl.ds(0, 64)] = d_down * alive
            even, odd = s2[pl.ds(b, 32, stride=2), :], s2[pl.ds(b + 1, 32, stride=2), :]
            d_even, d_odd = s2[pl.ds(b + 64, 32, stride=2), :], s2[pl.ds(b + 65, 32, stride=2), :]
            s1[pl.ds(j, 32, stride=GROUP), :] = jnp.where(low32, even, pltpu.roll(odd, 64, 1))
            s1[pl.ds(32 * GROUP + j, 32, stride=GROUP), :] = jnp.where(low32, pltpu.roll(even, 64, 1), odd)
            s1[pl.ds(64 * GROUP + j, 32, stride=GROUP), :] = jnp.where(low32, d_even, pltpu.roll(d_odd, 64, 1))
        rows = pl.ds(pl.multiple_of(g * GROUP, GROUP), GROUP)
        for i in range(SLOT // 128):
            raw[rows, pl.ds(i * 128, 128)] = s1[pl.ds(i * GROUP, GROUP), :].astype(BF16)
        return 0

    def cross_sum(n):
        for half in range(2):
            cols = piece(half, n, PIECES_B)
            collected(half, n, PIECES_B, rec_b, rb_recv)
            zsum[:, cols] = (
                part[4, :, cols].astype(F32) + rec_b[0, :, cols].astype(F32) + rec_b[1, :, cols].astype(F32)
            ).astype(BF16)
            send(zsum.at[:, cols], rsz.at[:, cols], z_send.at[half, n], z_recv.at[half, n], across)

    for n in range(PIECES_B):
        lax.fori_loop(n, n + 1, grads, 0)
        add_round(4, n, PIECES_B, hop_b, rec_b, rb_send, rb_hop, rb_recv)
    start_near(0, PIECES_A, rec_a, ra_send, ra_recv, 1)
    cross_sum(0)
    lax.fori_loop(4, 5, grads, 0)
    cross_sum(1)
    lax.fori_loop(5, 6, grads, 0)
    blocks_out = pltpu.make_async_copy(raw, block_grads, loc.at[2])
    blocks_out.start()
    cross_sum(2)
    cross_sum(3)
    for n in range(PIECES_A):
        for half in range(2):
            collected(half, n, PIECES_A, rec_a, ra_recv)
    outs = []
    for n in range(PIECES_B):
        for half in range(2):
            cols = piece(half, n, PIECES_B)
            total = part[0, :, cols].astype(F32) + rec_a[0, :, cols].astype(F32) + rec_a[1, :, cols].astype(F32)
            arrived(rsz.at[:, cols], z_recv.at[half, n])
            total = total + rsz[:, cols].astype(F32)
            ig[:, cols] = (dc[0, :, cols].astype(F32) + total).astype(BF16)
            copy = pltpu.make_async_copy(ig.at[:, cols], input_grad.at[:, cols], loc.at[3 + 2 * n + half])
            copy.start()
            outs.append(copy)

    for copy in pending:
        copy.wait_send()
    for p, cols in enumerate(PARTS):
        @pl.when(s > 0)
        def _():
            pltpu.make_async_remote_copy(
                src_ref=next_grad.at[:, cols], dst_ref=dc.at[0, :, cols], send_sem=sh_send.at[p],
                recv_sem=d_recv.at[0, 2 * p], device_id=before, device_id_type=MESH,
            ).wait_send()
    blocks_out.wait()
    for copy in outs:
        copy.wait()


def copy_kernel(a, b, a_out, b_out, a_buf, b_buf, sems):
    pairs = [(a, a_buf, a_out, pl.ds(0, TOK))]
    for n in range(CAP // GROUP):
        pairs.append((b, b_buf, b_out, pl.ds(n * GROUP, GROUP)))
    ins = [pltpu.make_async_copy(src.at[r], buf.at[r], sems.at[0, n]) for n, (src, buf, _, r) in enumerate(pairs)]
    outs = [pltpu.make_async_copy(buf.at[r], dst.at[r], sems.at[1, n]) for n, (_, buf, dst, r) in enumerate(pairs)]
    for copy in ins:
        copy.start()
    for into, out in zip(ins, outs):
        into.wait()
        out.start()
    for copy in outs:
        copy.wait()


def hand_over(input_grad, block_grads):
    any_space = pl.BlockSpec(memory_space=pl.ANY)
    input_grad, block_grads = pl.pallas_call(
        copy_kernel,
        out_shape=(
            jax.ShapeDtypeStruct(input_grad.shape, BF16),
            jax.ShapeDtypeStruct(block_grads.shape, BF16),
        ),
        in_specs=[any_space] * 2,
        out_specs=(any_space, any_space),
        scratch_shapes=[
            pltpu.VMEM(input_grad.shape, BF16),
            pltpu.VMEM(block_grads.shape, BF16),
            pltpu.SemaphoreType.DMA((2, 1 + CAP // GROUP)),
        ],
        compiler_params=pltpu.CompilerParams(vmem_limit_bytes=60 * 2**20),
    )(input_grad, block_grads)
    return input_grad[None], block_grads[None]


def per_device(sections, acts, next_grad, head_grad, blocks, block_row, block_col, live):
    index = pl.pallas_call(
        fill_table,
        out_shape=jax.ShapeDtypeStruct((16, 128), jnp.int32),
        in_specs=[pl.BlockSpec(memory_space=pltpu.SMEM)] + [pl.BlockSpec(memory_space=pltpu.VMEM)] * 2,
        out_specs=pl.BlockSpec(memory_space=pltpu.VMEM),
    )(live, block_row, block_col)
    dma = pltpu.SemaphoreType.DMA
    any_space = pl.BlockSpec(memory_space=pl.ANY)
    input_grad, block_grads = pl.pallas_call(
        functools.partial(kernel, sections),
        out_shape=(
            jax.ShapeDtypeStruct((TOK, WIDTH), BF16),
            jax.ShapeDtypeStruct((CAP, SLOT), BF16),
        ),
        in_specs=[pl.BlockSpec(memory_space=pltpu.SMEM)] + [any_space] * 4,
        out_specs=(any_space, any_space),
        scratch_shapes=[
            pltpu.VMEM((8, TOK, WIDTH), BF16),
            pltpu.VMEM((8, TOK, WIDTH), BF16),
            pltpu.VMEM((ROWS, 64, 2 * HALF), BF16),
            pltpu.VMEM((ROWS, 64, 2 * HALF), BF16),
            pltpu.VMEM((CAP, 128, 2 * HALF), BF16),
            pltpu.VMEM((CAP, 64, 2 * HALF), BF16),
            pltpu.VMEM((CAP + 1, 64, HALF), BF16),
            pltpu.VMEM((CAP, 64, 128), BF16),
            pltpu.VMEM((CAP, 192, 128), BF16),
            pltpu.VMEM((CAP, SLOT), BF16),
            pltpu.VMEM((8, TOK, WIDTH), BF16),
            pltpu.VMEM((2, TOK, WIDTH // 2), BF16),
            pltpu.VMEM((2, TOK, WIDTH // 2), BF16),
            pltpu.VMEM((2, TOK, WIDTH), BF16),
            pltpu.VMEM((2, TOK, WIDTH), BF16),
            pltpu.VMEM((TOK, WIDTH), BF16),
            pltpu.VMEM((TOK, WIDTH), BF16),
            pltpu.VMEM((SLOT // 128 * GROUP, 128), F32),
            pltpu.VMEM((4 * 192, 128), F32),
            pltpu.VMEM((192, HALF), F32),
            pltpu.VMEM((64, HALF), F32),
            pltpu.VMEM((TOK, WIDTH), BF16),
            dma((17,)),
            dma((17,)),
            dma((8, 4)),
            dma((8, 4)),
            dma((2,)),
            dma((6, PIECES_A)),
            dma((2, PIECES_A)),
            dma((2, 2, PIECES_A)),
            dma((6, PIECES_B)),
            dma((2, PIECES_B)),
            dma((2, 2, PIECES_B)),
            dma((2, PIECES_B)),
            dma((2, PIECES_B)),
            dma((3 + 2 * PIECES_B,)),
        ],
        compiler_params=pltpu.CompilerParams(
            collective_id=0, has_side_effects=True, vmem_limit_bytes=63 * 2**20
        ),
    )(index, acts[0], next_grad[0], head_grad, blocks[0])
    return hand_over(input_grad, block_grads)


def solution(mesh):
    return jax.shard_map(
        functools.partial(per_device, mesh.shape["section"]),
        mesh=mesh,
        in_specs=(
            P("section", "tensor", None),
            P("section", "tensor", None),
            P("tensor", None),
            P("section", "tensor", None),
            P("section", "tensor"),
            P("section", "tensor"),
            P("section", "tensor"),
        ),
        out_specs=(P("section", "tensor", None), P("section", "tensor", None)),
        check_vma=False,
    )
```

```python
import functools

import jax
import jax.numpy as jnp
from jax import lax
from jax.experimental import pallas as pl
from jax.experimental.pallas import tpu as pltpu
from jax.sharding import PartitionSpec as P

MESH = pl.DeviceIdType.MESH
BF16 = jnp.bfloat16
F32 = jnp.float32

CAP = 96
ROWS = 64
WIDTH = 4096
TOK = 64
HALF = 256
SLOT = 12288
GROUP = 16
SPLIT = 2048
REST = WIDTH - SPLIT

PARTS = (pl.ds(0, SPLIT), pl.ds(SPLIT, REST))
HALVES = (
    (pl.ds(0, SPLIT // 2), pl.ds(SPLIT // 2, SPLIT // 2)),
    (pl.ds(SPLIT, REST // 2), pl.ds(SPLIT + REST // 2, REST // 2)),
)

ORD_C, ROW_C, KEEP_C, ORD_R, POS_R, KEEP_R, LAST_R, POS_K, ROW_K, ALIVE = range(10)
PIECES_A, PIECES_B = 2, 4


def fill_table(live_ref, row_ref, col_ref, table):
    table[...] = jnp.zeros_like(table)
    lane = lax.broadcasted_iota(jnp.int32, (CAP, CAP), 1).astype(F32)
    sub = lax.broadcasted_iota(jnp.int32, (CAP, CAP), 0).astype(F32)
    one, none = jnp.ones((CAP, CAP), F32), jnp.zeros((CAP, CAP), F32)

    def both_ways(ref):
        along = jnp.broadcast_to(ref[...].astype(F32), (CAP, CAP))
        down = jnp.sum(jnp.where(lane == sub, along, none), axis=1, keepdims=True)
        return along, jnp.broadcast_to(down, (CAP, CAP))

    def sort(along, down):
        same = along == down
        ahead = jnp.where(same & (lane < sub), one, none)
        behind = jnp.where(same & (sub < lane), one, none)
        rank_down = jnp.sum(jnp.where(along < down, one, ahead), axis=1, keepdims=True)
        rank_along = jnp.sum(jnp.where(down < along, one, behind), axis=0, keepdims=True)
        follows = jnp.max(ahead, axis=1, keepdims=True)
        wide = jnp.broadcast_to(rank_down, (CAP, CAP))
        last_along = jnp.max(jnp.where(same, wide, none), axis=0, keepdims=True)
        last_down = jnp.max(
            jnp.where(same, jnp.broadcast_to(rank_along, (CAP, CAP)), none), axis=1, keepdims=True
        )
        return wide, jnp.broadcast_to(follows, (CAP, CAP)), last_along, jnp.broadcast_to(last_down, (CAP, CAP))

    row_along, row_down = both_ways(row_ref)
    col_along, col_down = both_ways(col_ref)
    rank_c, follows_c, last_along, last_down = sort(col_along, col_down)
    rank_r, follows_r, _, _ = sort(row_along, row_down)

    def put(place, values):
        table[pl.ds(place, 1), pl.ds(0, CAP)] = values.astype(jnp.int32)

    def in_order(rank, values):
        return jnp.sum(jnp.where(rank == lane, values, none), axis=0, keepdims=True)

    put(ORD_C, in_order(rank_c, sub))
    put(ROW_C, in_order(rank_c, row_down))
    put(KEEP_C, in_order(rank_c, follows_c))
    put(ORD_R, in_order(rank_r, sub))
    put(POS_R, in_order(rank_r, last_down))
    put(KEEP_R, in_order(rank_r, follows_r))
    ends = jnp.max(jnp.where(row_down == lane, rank_r + 1.0, none), axis=0, keepdims=True)
    put(LAST_R, jnp.where(ends == 0.0, jnp.full((1, CAP), CAP, F32), ends - 1.0))
    put(POS_K, last_along)
    put(ROW_K, row_along[:1])
    put(ALIVE, jnp.where(lane[:1] < live_ref[0, 0].astype(F32), one[:1], none[:1]))


def kernel(
    sections, index, acts, next_grad, head_grad, blocks, input_grad, block_grads,
    xc, dc, xt, dt, gu, hid, bk, wgu, wf, raw, part, hop_a, hop_b, rec_a, rec_b, rsz,
    zsum, s1, s2, acc, acc_b, ig,
    x_send, d_send, x_recv, d_recv, sh_send, ra_send, ra_hop, ra_recv, rb_send, rb_hop, rb_recv, z_send, z_recv, loc,
):
    s = lax.axis_index("section")
    t = lax.axis_index("tensor")
    y = lax.rem(t, 4)
    plane = t // 4

    def in_ring(step):
        return (s, plane * 4 + lax.rem(y + step, 4))

    across = (s, (1 - plane) * 4 + y)
    before = (lax.rem(s + sections - 1, sections), t)
    after = (lax.rem(s + 1, sections), t)

    barrier = pltpu.get_barrier_semaphore()
    for peer in (in_ring(1), in_ring(2), in_ring(3), across):
        pl.semaphore_signal(barrier, inc=1, device_id=peer, device_id_type=MESH)
    @pl.when(s < sections - 1)
    def _():
        pl.semaphore_signal(barrier, inc=1, device_id=after, device_id_type=MESH)

    blocks_in = pltpu.make_async_copy(blocks, raw, loc.at[0])
    blocks_in.start()
    own_in = pltpu.make_async_copy(acts, xc.at[0], loc.at[1])
    own_in.start()

    @pl.when(s > 0)
    def _():
        pl.semaphore_wait(barrier, 5)

    @pl.when(s == 0)
    def _():
        pl.semaphore_wait(barrier, 4)

    pending = []

    def send(src, dst, ssem, rsem, peer):
        copy = pltpu.make_async_remote_copy(
            src_ref=src, dst_ref=dst, send_sem=ssem, recv_sem=rsem, device_id=peer, device_id_type=MESH
        )
        copy.start()
        pending.append(copy)

    def arrived(dst, rsem):
        pltpu.make_async_remote_copy(
            src_ref=dst, dst_ref=dst, send_sem=rsem, recv_sem=rsem, device_id=across, device_id_type=MESH
        ).wait_recv()

    for p, cols in enumerate(PARTS):
        shift = pltpu.make_async_remote_copy(
            src_ref=next_grad.at[:, cols], dst_ref=dc.at[0, :, cols], send_sem=sh_send.at[p],
            recv_sem=d_recv.at[0, 2 * p], device_id=before, device_id_type=MESH,
        )

        @pl.when(s > 0)
        def _():
            shift.start()

        @pl.when(s == sections - 1)
        def _():
            pltpu.make_async_copy(head_grad.at[:, cols], dc.at[0, :, cols], d_recv.at[0, 2 * p]).start()

    def share_own(src, buf, ssem, rsem):
        for p, cols in enumerate(PARTS):
            send(src.at[:, cols], buf.at[4, :, cols], ssem.at[p], rsem.at[4, 2 * p], across)
            for step in (1, 3):
                send(
                    src.at[:, cols], buf.at[4 - step, :, cols], ssem.at[step + 1 + p], rsem.at[4 - step, 2 * p],
                    in_ring(step),
                )

    def round_own(buf, ssem, rsem):
        for p in (1, 0):
            for way, (place, step) in enumerate(((3, 1), (1, 3))):
                arrived(buf.at[place, :, PARTS[p]], rsem.at[place, 2 * p])
                cols = HALVES[p][way]
                send(
                    buf.at[place, :, cols], buf.at[2, :, cols], ssem.at[6 + 2 * p + way], rsem.at[2, 2 * p + way],
                    in_ring(step),
                )
        for place in (1, 3):
            cols = PARTS[1]
            send(
                buf.at[place, :, cols], buf.at[4 + place, :, cols], ssem.at[10 + place // 2], rsem.at[4 + place, 2],
                across,
            )

    def share_first(buf, ssem, rsem):
        cols = PARTS[0]
        arrived(buf.at[4, :, cols], rsem.at[4, 0])
        for step in (1, 3):
            send(
                buf.at[4, :, cols], buf.at[8 - step, :, cols], ssem.at[12 + step // 2], rsem.at[8 - step, 0],
                in_ring(step),
            )

    def cross_last(buf, ssem, rsem):
        for p in range(2):
            for way in range(2):
                arrived(buf.at[2, :, HALVES[p][way]], rsem.at[2, 2 * p + way])
        send(buf.at[2, :, PARTS[1]], buf.at[6, :, PARTS[1]], ssem.at[14], rsem.at[6, 2], across)

    def round_first(buf, ssem, rsem):
        for way, (place, step) in enumerate(((7, 1), (5, 3))):
            arrived(buf.at[place, :, PARTS[0]], rsem.at[place, 0])
            cols = HALVES[0][way]
            send(buf.at[place, :, cols], buf.at[6, :, cols], ssem.at[15 + way], rsem.at[6, way], in_ring(step))

    def rest_near(buf, rsem):
        for place in (5, 7):
            arrived(buf.at[place, :, PARTS[1]], rsem.at[place, 2])

    def rest_far(buf, rsem):
        for place in (4, 6):
            arrived(buf.at[place, :, PARTS[1]], rsem.at[place, 2])
        for way in range(2):
            arrived(buf.at[6, :, HALVES[0][way]], rsem.at[6, way])

    share_own(acts, xc, x_send, x_recv)

    blocks_in.wait()
    low = lax.broadcasted_iota(jnp.int32, (64, 128), 1) < 64
    low32 = lax.broadcasted_iota(jnp.int32, (32, 128), 1) < 64

    def prepare(g, _):
        rows = pl.ds(pl.multiple_of(g * GROUP, GROUP), GROUP)
        for i in range(SLOT // 128):
            s1[pl.ds(i * GROUP, GROUP), :] = raw[rows, pl.ds(i * 128, 128)].astype(F32)
        for j in range(GROUP):
            k = g * GROUP + j
            b = (j % 4) * 192
            for m in range(3):
                v = s1[pl.ds(m * 32 * GROUP + j, 32, stride=GROUP), :]
                turned = pltpu.roll(v, 64, 1)
                even, odd = (turned, v) if m == 1 else (v, turned)
                s2[pl.ds(b + m * 64, 32, stride=2), :] = even
                s2[pl.ds(b + m * 64 + 1, 32, stride=2), :] = odd
            both = jnp.where(low, s2[pl.ds(b, 64), :], s2[pl.ds(b + 64, 64), :])
            alive = index[ALIVE, k].astype(F32)
            both = both * alive
            down = s2[pl.ds(b + 128, 64), :] * alive
            wgu[k] = both.astype(BF16)
            wf[k, pl.ds(0, 128), pl.ds(0, 64)] = both.T.astype(BF16)
            wf[k, pl.ds(0, 128), pl.ds(64, 64)] = jnp.zeros((128, 64), BF16)
            wf[k, pl.ds(128, 64), :] = jnp.where(low, 0.0, pltpu.roll(down, 64, 1)).astype(BF16)
        return 0

    lax.fori_loop(0, CAP // GROUP // 2, prepare, 0)

    for p, cols in enumerate(PARTS):
        arrived(dc.at[0, :, cols], d_recv.at[0, 2 * p])
    share_own(dc.at[0], dc, d_send, d_recv)
    lax.fori_loop(CAP // GROUP // 2, CAP // GROUP, prepare, 0)
    bk[CAP] = jnp.zeros((64, HALF), BF16)

    def turn(buf, out, pair, first, second):
        def step(i, _):
            cols = pl.ds(pl.multiple_of(i * 128, 128), 128)
            tile = jnp.concatenate([buf[first, :, cols], buf[second, :, cols]], axis=0)
            tile = tile.T
            out[2 * i, :, pl.ds(pair * 128, 128)] = tile[:64]
            out[2 * i + 1, :, pl.ds(pair * 128, 128)] = tile[64:]
            return 0

        lax.fori_loop(0, WIDTH // 128, step, 0, unroll=4)

    def forward(start, width):
        lanes, here = pl.ds(start, width), pl.ds(0, width)
        acc[...] = jnp.zeros_like(acc)

        def step(i, _):
            slots = [2 * i, 2 * i + 1]
            tokens, weights = [], []
            for j in slots:
                r = index[ROW_C, j]
                tokens += [xt[r, :, lanes], dt[r, :, lanes]]
                weights.append(wf[index[ORD_C, j]])
            none = jnp.zeros((192, 128), BF16)
            weights = jnp.concatenate(
                [jnp.concatenate([weights[0], none], axis=1), jnp.concatenate([none, weights[1]], axis=1)], axis=0
            )
            new = jnp.dot(weights, jnp.concatenate(tokens, axis=0), preferred_element_type=F32)
            total = acc[:, here]
            for n, j in enumerate(slots):
                total = new[n * 192:(n + 1) * 192] + index[KEEP_C, j].astype(F32) * total
                gate, upper, hg = total[:64], total[64:128], total[128:]
                sg = 0.5 + 0.5 * jnp.tanh(0.5 * gate)
                act = gate * sg
                hid[j, :, lanes] = (act * upper).astype(BF16)
                gu[j, pl.ds(0, 64), lanes] = (hg * upper * sg * (1.0 + gate * (1.0 - sg))).astype(BF16)
                gu[j, pl.ds(64, 64), lanes] = (hg * act).astype(BF16)
            acc[:, here] = total
            return 0

        lax.fori_loop(0, CAP // 2, step, 0, unroll=4 * HALF // width)

    def backward(start, width, pairs):
        lanes, here = pl.ds(start, width), pl.ds(0, width)
        acc_b[...] = jnp.zeros_like(acc_b)

        def step(i, _):
            slots = [2 * i, 2 * i + 1]
            none = jnp.zeros((64, 128), BF16)
            first, second = (wgu[index[ORD_R, j]] for j in slots)
            weights = jnp.concatenate(
                [jnp.concatenate([first, none], axis=1), jnp.concatenate([none, second], axis=1)], axis=0
            )
            both = jnp.concatenate([gu[index[POS_R, j], :, lanes] for j in slots], axis=0)
            new = jnp.dot(weights, both, preferred_element_type=F32)
            total = acc_b[:, here]
            for n, j in enumerate(slots):
                total = new[n * 64:(n + 1) * 64] + index[KEEP_R, j].astype(F32) * total
                bk[j, :, here] = total.astype(BF16)
            acc_b[:, here] = total
            return 0

        lax.fori_loop(0, CAP // 2, step, 0, unroll=4 * HALF // width)

        def place(i, _):
            cols = pl.ds(pl.multiple_of(i * 128, 128), 128)
            both = jnp.concatenate(
                [bk[index[LAST_R, 2 * i], :, here], bk[index[LAST_R, 2 * i + 1], :, here]], axis=0
            )
            for q, (first, second) in enumerate(pairs):
                tile = both[:, q * 128:(q + 1) * 128].T
                part[first, :, cols] = tile[:64]
                part[second, :, cols] = tile[64:]
            return 0

        lax.fori_loop(0, ROWS // 2, place, 0, unroll=2)

    def piece(half, n, pieces):
        return pl.ds(half * WIDTH // 2 + n * (WIDTH // 2 // pieces), WIDTH // 2 // pieces)

    def start_far(base, pieces, hop, ssem, hsem):
        for n in range(pieces):
            for way, step in enumerate((1, 3)):
                send(
                    part.at[base + 2, :, piece(way, n, pieces)], hop.at[way, :, piece(0, n, pieces)],
                    ssem.at[way, n], hsem.at[way, n], in_ring(step),
                )

    def start_near(base, pieces, rec, ssem, rsem, first=0, end=None):
        for n in range(first, pieces if end is None else end):
            for way, step in enumerate((1, 3)):
                cols = piece(1 - way, n, pieces)
                send(
                    part.at[base + step, :, cols], rec.at[way, :, cols], ssem.at[2 + way, n],
                    rsem.at[way, 1 - way, n], in_ring(step),
                )

    def add_round(base, n, pieces, hop, rec, ssem, hsem, rsem):
        here = piece(0, n, pieces)
        for way, step in enumerate((1, 3)):
            cols = piece(way, n, pieces)
            arrived(hop.at[way, :, here], hsem.at[way, n])
            part[base + step, :, cols] = (
                part[base + step, :, cols].astype(F32) + hop[way, :, here].astype(F32)
            ).astype(BF16)
            send(part.at[base + step, :, cols], rec.at[way, :, cols], ssem.at[4 + way, n], rsem.at[way, way, n], in_ring(step))

    def collected(half, n, pieces, rec, rsem):
        for way in range(2):
            arrived(rec.at[way, :, piece(half, n, pieces)], rsem.at[way, half, n])

    own_in.wait()
    round_own(xc, x_send, x_recv)
    share_first(xc, x_send, x_recv)
    turn(xc, xt, 0, 0, 1)
    round_own(dc, d_send, d_recv)
    share_first(dc, d_send, d_recv)
    turn(dc, dt, 0, 0, 1)
    cross_last(xc, x_send, x_recv)
    turn(xc, xt, 1, 2, 3)
    cross_last(dc, d_send, d_recv)
    turn(dc, dt, 1, 2, 3)
    forward(0, HALF)
    round_first(xc, x_send, x_recv)
    backward(0, HALF, ((0, 1), (2, 3)))
    round_first(dc, d_send, d_recv)
    start_far(0, PIECES_A, hop_a, ra_send, ra_hop)
    start_near(0, PIECES_A, rec_a, ra_send, ra_recv, 0, 1)

    rest_near(xc, x_recv)
    turn(xc, xt, 2, 5, 7)
    rest_near(dc, d_recv)
    turn(dc, dt, 2, 5, 7)
    forward(HALF, HALF // 2)
    add_round(0, 0, PIECES_A, hop_a, rec_a, ra_send, ra_hop, ra_recv)
    backward(HALF, HALF // 2, ((5, 7),))
    start_near(4, PIECES_B, rec_b, rb_send, rb_recv)
    add_round(0, 1, PIECES_A, hop_a, rec_a, ra_send, ra_hop, ra_recv)
    rest_far(xc, x_recv)
    turn(xc, xt, 3, 4, 6)
    rest_far(dc, d_recv)
    turn(dc, dt, 3, 4, 6)
    forward(HALF + HALF // 2, HALF // 2)
    backward(HALF + HALF // 2, HALF // 2, ((4, 6),))
    start_far(4, PIECES_B, hop_b, rb_send, rb_hop)

    def grads(g, _):
        for j in range(GROUP):
            k = g * GROUP + j
            p, r = index[POS_K, k], index[ROW_K, k]
            alive = index[ALIVE, k].astype(F32)
            turned = (((1,), (1,)), ((), ()))
            d_both = lax.dot_general(xt[r], gu[p], turned, preferred_element_type=F32)
            d_down = lax.dot_general(hid[p], dt[r], turned, preferred_element_type=F32)
            b = (j % 4) * 192
            s2[pl.ds(b, 64), :] = d_both * alive
            s2[pl.ds(b + 64, 64), pl.ds(0, 64)] = d_down * alive
            even, odd = s2[pl.ds(b, 32, stride=2), :], s2[pl.ds(b + 1, 32, stride=2), :]
            d_even, d_odd = s2[pl.ds(b + 64, 32, stride=2), :], s2[pl.ds(b + 65, 32, stride=2), :]
            s1[pl.ds(j, 32, stride=GROUP), :] = jnp.where(low32, even, pltpu.roll(odd, 64, 1))
            s1[pl.ds(32 * GROUP + j, 32, stride=GROUP), :] = jnp.where(low32, pltpu.roll(even, 64, 1), odd)
            s1[pl.ds(64 * GROUP + j, 32, stride=GROUP), :] = jnp.where(low32, d_even, pltpu.roll(d_odd, 64, 1))
        rows = pl.ds(pl.multiple_of(g * GROUP, GROUP), GROUP)
        for i in range(SLOT // 128):
            raw[rows, pl.ds(i * 128, 128)] = s1[pl.ds(i * GROUP, GROUP), :].astype(BF16)
        return 0

    def cross_sum(n):
        for half in range(2):
            cols = piece(half, n, PIECES_B)
            collected(half, n, PIECES_B, rec_b, rb_recv)
            zsum[:, cols] = (
                part[4, :, cols].astype(F32) + rec_b[0, :, cols].astype(F32) + rec_b[1, :, cols].astype(F32)
            ).astype(BF16)
            send(zsum.at[:, cols], rsz.at[:, cols], z_send.at[half, n], z_recv.at[half, n], across)

    for n in range(PIECES_B):
        lax.fori_loop(n, n + 1, grads, 0)
        add_round(4, n, PIECES_B, hop_b, rec_b, rb_send, rb_hop, rb_recv)
    start_near(0, PIECES_A, rec_a, ra_send, ra_recv, 1)
    cross_sum(0)
    lax.fori_loop(4, 5, grads, 0)
    cross_sum(1)
    lax.fori_loop(5, 6, grads, 0)
    blocks_out = pltpu.make_async_copy(raw, block_grads, loc.at[2])
    blocks_out.start()
    cross_sum(2)
    cross_sum(3)
    for n in range(PIECES_A):
        for half in range(2):
            collected(half, n, PIECES_A, rec_a, ra_recv)
    outs = []
    for n in range(PIECES_B):
        for half in range(2):
            cols = piece(half, n, PIECES_B)
            total = part[0, :, cols].astype(F32) + rec_a[0, :, cols].astype(F32) + rec_a[1, :, cols].astype(F32)
            arrived(rsz.at[:, cols], z_recv.at[half, n])
            total = total + rsz[:, cols].astype(F32)
            ig[:, cols] = (dc[0, :, cols].astype(F32) + total).astype(BF16)
            copy = pltpu.make_async_copy(ig.at[:, cols], input_grad.at[:, cols], loc.at[3 + 2 * n + half])
            copy.start()
            outs.append(copy)

    for copy in pending:
        copy.wait_send()
    for p, cols in enumerate(PARTS):
        @pl.when(s > 0)
        def _():
            pltpu.make_async_remote_copy(
                src_ref=next_grad.at[:, cols], dst_ref=dc.at[0, :, cols], send_sem=sh_send.at[p],
                recv_sem=d_recv.at[0, 2 * p], device_id=before, device_id_type=MESH,
            ).wait_send()
    blocks_out.wait()
    for copy in outs:
        copy.wait()


def copy_kernel(a, b, a_out, b_out, a_buf, b_buf, sems):
    pairs = [(a, a_buf, a_out, pl.ds(0, TOK))]
    for n in range(CAP // GROUP):
        pairs.append((b, b_buf, b_out, pl.ds(n * GROUP, GROUP)))
    ins = [pltpu.make_async_copy(src.at[r], buf.at[r], sems.at[0, n]) for n, (src, buf, _, r) in enumerate(pairs)]
    outs = [pltpu.make_async_copy(buf.at[r], dst.at[r], sems.at[1, n]) for n, (_, buf, dst, r) in enumerate(pairs)]
    for copy in ins:
        copy.start()
    for into, out in zip(ins, outs):
        into.wait()
        out.start()
    for copy in outs:
        copy.wait()


def hand_over(input_grad, block_grads):
    any_space = pl.BlockSpec(memory_space=pl.ANY)
    input_grad, block_grads = pl.pallas_call(
        copy_kernel,
        out_shape=(
            jax.ShapeDtypeStruct(input_grad.shape, BF16),
            jax.ShapeDtypeStruct(block_grads.shape, BF16),
        ),
        in_specs=[any_space] * 2,
        out_specs=(any_space, any_space),
        scratch_shapes=[
            pltpu.VMEM(input_grad.shape, BF16),
            pltpu.VMEM(block_grads.shape, BF16),
            pltpu.SemaphoreType.DMA((2, 1 + CAP // GROUP)),
        ],
        compiler_params=pltpu.CompilerParams(vmem_limit_bytes=60 * 2**20),
    )(input_grad, block_grads)
    return input_grad[None], block_grads[None]


def per_device(sections, acts, next_grad, head_grad, blocks, block_row, block_col, live):
    index = pl.pallas_call(
        fill_table,
        out_shape=jax.ShapeDtypeStruct((16, 128), jnp.int32),
        in_specs=[pl.BlockSpec(memory_space=pltpu.SMEM)] + [pl.BlockSpec(memory_space=pltpu.VMEM)] * 2,
        out_specs=pl.BlockSpec(memory_space=pltpu.VMEM),
    )(live, block_row, block_col)
    dma = pltpu.SemaphoreType.DMA
    any_space = pl.BlockSpec(memory_space=pl.ANY)
    input_grad, block_grads = pl.pallas_call(
        functools.partial(kernel, sections),
        out_shape=(
            jax.ShapeDtypeStruct((TOK, WIDTH), BF16),
            jax.ShapeDtypeStruct((CAP, SLOT), BF16),
        ),
        in_specs=[pl.BlockSpec(memory_space=pltpu.SMEM)] + [any_space] * 4,
        out_specs=(any_space, any_space),
        scratch_shapes=[
            pltpu.VMEM((8, TOK, WIDTH), BF16),
            pltpu.VMEM((8, TOK, WIDTH), BF16),
            pltpu.VMEM((ROWS, 64, 2 * HALF), BF16),
            pltpu.VMEM((ROWS, 64, 2 * HALF), BF16),
            pltpu.VMEM((CAP, 128, 2 * HALF), BF16),
            pltpu.VMEM((CAP, 64, 2 * HALF), BF16),
            pltpu.VMEM((CAP + 1, 64, HALF), BF16),
            pltpu.VMEM((CAP, 64, 128), BF16),
            pltpu.VMEM((CAP, 192, 128), BF16),
            pltpu.VMEM((CAP, SLOT), BF16),
            pltpu.VMEM((8, TOK, WIDTH), BF16),
            pltpu.VMEM((2, TOK, WIDTH // 2), BF16),
            pltpu.VMEM((2, TOK, WIDTH // 2), BF16),
            pltpu.VMEM((2, TOK, WIDTH), BF16),
            pltpu.VMEM((2, TOK, WIDTH), BF16),
            pltpu.VMEM((TOK, WIDTH), BF16),
            pltpu.VMEM((TOK, WIDTH), BF16),
            pltpu.VMEM((SLOT // 128 * GROUP, 128), F32),
            pltpu.VMEM((4 * 192, 128), F32),
            pltpu.VMEM((192, HALF), F32),
            pltpu.VMEM((64, HALF), F32),
            pltpu.VMEM((TOK, WIDTH), BF16),
            dma((17,)),
            dma((17,)),
            dma((8, 4)),
            dma((8, 4)),
            dma((2,)),
            dma((6, PIECES_A)),
            dma((2, PIECES_A)),
            dma((2, 2, PIECES_A)),
            dma((6, PIECES_B)),
            dma((2, PIECES_B)),
            dma((2, 2, PIECES_B)),
            dma((2, PIECES_B)),
            dma((2, PIECES_B)),
            dma((3 + 2 * PIECES_B,)),
        ],
        compiler_params=pltpu.CompilerParams(
            collective_id=0, has_side_effects=True, vmem_limit_bytes=63 * 2**20
        ),
    )(index, acts[0], next_grad[0], head_grad, blocks[0])
    return hand_over(input_grad, block_grads)


def solution(mesh):
    return jax.shard_map(
        functools.partial(per_device, mesh.shape["section"]),
        mesh=mesh,
        in_specs=(
            P("section", "tensor", None),
            P("section", "tensor", None),
            P("tensor", None),
            P("section", "tensor", None),
            P("section", "tensor"),
            P("section", "tensor"),
            P("section", "tensor"),
        ),
        out_specs=(P("section", "tensor", None), P("section", "tensor", None)),
        check_vma=False,
    )
```
